32 devices in a mesh: section: 8 (over z, core), dp: 4 (over y, x).
Axes of the slice: x: 2, y: 2, z: 4, core: 2. Of those that a mesh axis runs over, the one named last changes fastest.
Arguments:
- first_acts: bfloat16 [8, 512, 8192], P('section', 'dp'), may hold values from -6 to 6
- first_grads: bfloat16 [8, 512, 8192], P('section', 'dp'), may hold values from -6 to 6
- last_acts: bfloat16 [8, 512, 8192], P('section', 'dp'), may hold values from -6 to 6
- last_grads: bfloat16 [8, 512, 8192], P('section', 'dp'), may hold values from -6 to 6
- doc_lengths: int32 [4, 16], P('dp'), may hold values from 1 to 32, 128 in all within a row
- block_owner: int32 [16], replicated, may hold values from 0 to 3, as said below
Outputs:
- act_factor: float32 [8, 4, 8, 512, 512], P('section', 'dp')
- grad_factor: float32 [8, 4, 8, 512, 512], P('section', 'dp')
- act_cross: float32 [8, 4, 8, 512, 512], P('section', 'dp')
- grad_cross: float32 [8, 4, 8, 512, 512], P('section', 'dp')
The draws below stay inside these ranges and needn't reach their ends.
Inputs may be any that keep to these rules, and one draw needn't show every extreme that they name: `doc_lengths`: documents fill their group's 128 rows exactly and the longest is exactly 32 rows. `block_owner`: one owner holds exactly 8 blocks, one holds none, every other holds exactly 4; which ones is drawn, except that the first and the last group always own blocks.
All inputs are finite; a program needn't handle non-finite values.
Results may differ from the reference program's by a relative error of at most 0.0037.
Values may be sent and summed in bfloat16 or wider, within the bound.
A program may use at most 320 MiB of HBM per device.

```python
import math
import jax
import jax.numpy as jnp
import numpy as np
from jax import lax

D = 8192
FB = 512
TOK_DEV = 128
DOCS = 16
SECTIONS = 8
GROUPS = 4
TOKENS = 512
TOTAL_DOCS = 64
DOC_MOST = 32
BLOCKS = 16
OWNED = 4
MOST_OWNED = 8


def draw_block_owner(key, part):
    owners = BLOCKS // OWNED
    pattern = np.concatenate([np.zeros(MOST_OWNED, dtype=np.int32), np.repeat(np.arange(2, owners, dtype=np.int32), OWNED)])
    ranking = jax.random.permutation(jax.random.fold_in(key, 11), owners).astype(jnp.int32)
    middle_one = (ranking[1] > 0) & (ranking[1] < owners - 1)
    middle_two = (ranking[2] > 0) & (ranking[2] < owners - 1)
    pick = jnp.where(middle_one, 1, jnp.where(middle_two, 2, 3)).astype(jnp.int32)
    value_one = ranking[1]
    value_pick = ranking[pick]
    ranking = ranking.at[pick].set(value_one)
    ranking = ranking.at[1].set(value_pick)
    shuffle = jax.random.permutation(jax.random.fold_in(key, 12), BLOCKS)
    return ranking[jnp.asarray(pattern)[shuffle]].astype(jnp.int32)


def block_levels(own_key, shape, pieces, smallest, largest):
    def one(axis_at, blocks):
        draws = jax.random.uniform(jax.random.fold_in(jax.random.fold_in(own_key, 6), axis_at), (blocks,), jnp.float32, smallest / len(pieces), largest / len(pieces))
        return jnp.repeat(jnp.exp(draws), shape[axis_at] // blocks).reshape((-1,) + (1,) * (len(shape) - axis_at - 1))

    gain = one(*pieces[0])
    for cut in pieces[1:]:
        gain = gain * one(*cut)
    return gain


def length_profile(count, total, most, skew):
    loads = [(1 << 20) // math.isqrt(grade ** skew) + 1 for grade in range(2, count + 1)]
    spare, counts = total - most - (count - 1), [1] * (count - 1)
    while spare > 0:
        candidates = [i for i in range(count - 1) if counts[i] < most]
        whole, budget = sum([loads[i] for i in candidates]), spare
        for i in candidates:
            addition = min(most - counts[i], max(1, budget * loads[i] // whole), spare)
            counts[i] = counts[i] + addition
            spare = spare - addition
    return np.array([most] + counts)


def uneven(key, number_of, total, reach, lean):
    if number_of == 2:
        one = jax.random.randint(key, (), max(1, total - reach), min(reach, total - 1) + 1)
        return jnp.stack([one, total - one])
    tallies = jnp.asarray(length_profile(number_of, total, reach, lean), jnp.int32)
    twos = (number_of - 1) // 2
    giver, receiver = tallies[1:1 + 2 * twos:2], tallies[2:2 + 2 * twos:2]
    room = jnp.minimum(giver - 1, reach - receiver)
    shifted = jax.random.randint(jax.random.fold_in(key, 1), (twos,), 0, 1 << 20) % (room + 1)
    tallies = tallies.at[1:1 + 2 * twos:2].set(giver - shifted).at[2:2 + 2 * twos:2].set(receiver + shifted)
    return tallies[jax.random.permutation(jax.random.fold_in(key, 2), number_of)]


def gaussian(own_key, dims, width, bound, split=(), kind=jnp.bfloat16):
    array = width * jax.random.normal(own_key, dims, jnp.float32)
    if split:
        array = array * block_levels(own_key, dims, split, -0.22, 0.18)
    return jnp.clip(array, -bound, bound).astype(kind)


def setup_inputs(seed: int = 0) -> dict:
    splits = jax.random.split(jax.random.key(seed), 7)
    first_acts = gaussian(splits[0], (SECTIONS, TOKENS, D), 1.0, 6.0, ((0, 8), (1, 4)))
    first_grads = gaussian(splits[1], (SECTIONS, TOKENS, D), 1.0, 6.0, ((0, 8), (1, 4)))
    last_acts = gaussian(splits[2], (SECTIONS, TOKENS, D), 1.0, 6.0, ((0, 8), (1, 4)))
    last_grads = gaussian(splits[3], (SECTIONS, TOKENS, D), 1.0, 6.0, ((0, 8), (1, 4)))
    doc_lengths = jax.vmap(lambda own: uneven(own, DOCS, TOK_DEV, DOC_MOST, 2))(jax.random.split(splits[4], GROUPS)).reshape((GROUPS, DOCS)).astype(jnp.int32)
    block_owner = draw_block_owner(jax.random.fold_in(splits[6], 71), 0)
    return dict(first_acts=first_acts, first_grads=first_grads, last_acts=last_acts, last_grads=last_grads, doc_lengths=doc_lengths, block_owner=block_owner)


def row_scale(doc_lengths):
    doc_sizes = doc_lengths.astype(jnp.float32)
    doc_end = jnp.cumsum(doc_lengths, axis=1)
    starts = doc_end - doc_lengths
    places = jnp.arange(TOK_DEV, dtype=jnp.int32)
    inside = (places[None, :, None] >= starts[:, None, :]) & (places[None, :, None] < doc_end[:, None, :])
    inverse = lax.optimization_barrier(jnp.sum(jnp.where(inside, 1.0 / doc_sizes[:, None, :], jnp.float32(0.0)), axis=2))
    return jnp.sqrt(inverse / TOTAL_DOCS).reshape(TOKENS)

def slot_order(block_owner):
    position = jnp.arange(BLOCKS, dtype=jnp.int32)
    same_owner = block_owner[:, None] == block_owner[None, :]
    earlier = position[None, :] < position[:, None]
    return lax.optimization_barrier(jnp.sum(jnp.where(same_owner & earlier, 1, 0), axis=1)).astype(jnp.int32)

def block_grams(former, latter):
    first_rows = former.astype(jnp.float32).reshape(TOKENS, BLOCKS, FB)
    second_rows = latter.astype(jnp.float32).reshape(TOKENS, BLOCKS, FB)
    return jnp.einsum('tbf,tbg->bfg', first_rows, second_rows, precision=lax.Precision.HIGHEST)

def place_slots(grams, block_owner, slot_index):
    empty = jnp.zeros((GROUPS, MOST_OWNED, FB, FB), jnp.float32)
    return empty.at[block_owner, slot_index].set(grams)

def reference(first_acts, first_grads, last_acts, last_grads, doc_lengths, block_owner):
    row_weight = row_scale(doc_lengths)[:, None]
    slot_index = slot_order(block_owner)

    def weighted(matrix):
        return (matrix.astype(jnp.float32) * row_weight).astype(jnp.bfloat16)

    def one_section(section_index):
        before = jnp.maximum(section_index - 1, 0)
        has_prev = jnp.where(section_index > 0, 1.0, 0.0).astype(jnp.float32)
        own_acts = weighted(first_acts[section_index])
        own_grads = weighted(first_grads[section_index])
        prev_acts = weighted(last_acts[before])
        prev_grads = weighted(last_grads[before])
        first = place_slots(block_grams(own_acts, own_acts), block_owner, slot_index)
        second = place_slots(block_grams(own_grads, own_grads), block_owner, slot_index)
        third = place_slots(block_grams(prev_acts, own_acts), block_owner, slot_index) * has_prev
        fourth = place_slots(block_grams(prev_grads, own_grads), block_owner, slot_index) * has_prev
        return (first, second, third, fourth)
    act_factor, grad_factor, act_cross, grad_cross = lax.map(one_section, jnp.arange(SECTIONS, dtype=jnp.int32))
    return (act_factor, grad_factor, act_cross, grad_cross)
```

```python
import functools

import jax
import jax.numpy as jnp
from jax import lax
from jax.experimental import pallas as pl
from jax.experimental.pallas import tpu as pltpu
from jax.sharding import PartitionSpec as P

MESH = pl.DeviceIdType.MESH

ACROSS = {0: {1: 2, 2: 2}, 1: {1: 0, 2: 4}, 2: {1: 4, 2: 0}, 3: {1: 4, 2: 4}}


def held_at(place):
    return 8 if place == 0 else 4


def base_of(place):
    return 0 if place == 0 else 8 + 4 * (place - 1)


def across_part(place, link):
    return (0 if link == 1 else ACROSS[place][1]), ACROSS[place][link]


def arrange_kernel(order_ref, lengths_ref, fa_ref, fg_ref, la_ref, lg_ref, first_ref, last_ref, weight):
    docs = lengths_ref.shape[0]
    rows = fa_ref.shape[1]

    @pl.when(pl.program_id(0) == 0)
    def _():
        place = lax.broadcasted_iota(jnp.int32, (rows, 128), 0)
        length = jnp.ones((rows, 128), jnp.int32)
        start = jnp.int32(0)
        for d in range(docs):
            size = lengths_ref[d]
            length = jnp.where((place >= start) & (place < start + size), size, length)
            start = start + size
        weight[...] = jnp.sqrt((1.0 / length.astype(jnp.float32)) / weight_docs(docs))

    row_weight = weight[:, 0:1]
    for half, ref in ((0, fa_ref), (1, fg_ref)):
        first_ref[half, 0] = (ref[0].astype(jnp.float32) * row_weight).astype(jnp.bfloat16)
    for half, ref in ((0, la_ref), (1, lg_ref)):
        last_ref[half, 0] = (ref[0].astype(jnp.float32) * row_weight).astype(jnp.bfloat16)


def weight_docs(docs):
    return jnp.float32(docs * 4)


def arrange(order, lengths, arrays, width):
    rows = arrays[0].shape[1]
    count = order.shape[0]
    in_spec = pl.BlockSpec((1, rows, width), lambda i, order, lengths: (0, 0, order[i]))
    out_spec = pl.BlockSpec((2, 1, rows, width), lambda i, order, lengths: (0, i, 0, 0))
    shape = jax.ShapeDtypeStruct((2, count, rows, width), jnp.bfloat16)
    return pl.pallas_call(
        arrange_kernel,
        grid_spec=pltpu.PrefetchScalarGridSpec(
            num_scalar_prefetch=2,
            grid=(count,),
            in_specs=[in_spec] * 4,
            out_specs=[out_spec] * 2,
            scratch_shapes=[pltpu.VMEM((rows, 128), jnp.float32)],
        ),
        out_shape=(shape, shape),
        compiler_params=pltpu.CompilerParams(vmem_limit_bytes=32 * 2**20),
        name="arrange",
    )(order, lengths, *arrays)


def exchange_kernel(
    most, sections, first, last, got_first, got_last, moved, relay, send_sem, recv_sem, move_send, move_recv
):
    me = lax.axis_index("dp")
    section = lax.axis_index("section")
    has_prev = section > 0
    has_next = section < sections - 1

    def move(half):
        return pltpu.make_async_remote_copy(
            src_ref=last.at[half],
            dst_ref=moved.at[half],
            send_sem=move_send.at[half],
            recv_sem=move_recv.at[half],
            device_id={"section": section + 1},
            device_id_type=MESH,
        )

    def role(place):
        def peer(link):
            return {"dp": most ^ place ^ link}

        def source(a):
            return first.at[a] if a < 2 else moved.at[a - 2]

        def target(a):
            return got_first.at[a] if a < 2 else got_last.at[a - 2]

        def copy(src, dst, a, sent, received, link):
            return pltpu.make_async_remote_copy(
                src_ref=src,
                dst_ref=dst,
                send_sem=send_sem.at[a, sent],
                recv_sem=recv_sem.at[a, received],
                device_id=peer(link),
                device_id_type=MESH,
            )

        def direct(a, link):
            to = place ^ link
            n = held_at(to)
            src = source(a).at[pl.ds(base_of(to), n)]
            return copy(src, target(a).at[link - 1, pl.ds(0, n)], a, link - 1, link - 1, link)

        def hop(a, link):
            offset, n = across_part(place, link)
            src = source(a).at[pl.ds(base_of(place ^ 3) + offset, n)]
            return copy(src, relay.at[a, link - 1, pl.ds(0, n)], a, 1 + link, 1 + link, link)

        def forward(a, link):
            offset, n = across_part(place ^ link, link)
            src = relay.at[a, link - 1, pl.ds(0, n)]
            out = 3 - link
            return copy(src, target(a).at[2, pl.ds(offset, n)], a, 3 + link, 3 + out, out)

        def arrival(dst, a, received):
            return copy(dst, dst, a, received, received, 1)

        def wait_hop(a, link):
            n = across_part(place ^ link, link)[1]
            arrival(relay.at[a, link - 1, pl.ds(0, n)], a, 1 + link).wait_recv()

        def sends(a):
            return [link for link in (1, 2) if ACROSS[place][link]]

        def relays(a):
            return [link for link in (1, 2) if ACROSS[place ^ link][link]]

        def start(a):
            for link in sends(a):
                hop(a, link).start()
            for link in (1, 2):
                direct(a, link).start()

        def pass_on(a):
            for link in relays(a):
                wait_hop(a, link)
                forward(a, link).start()

        def finish(a):
            n = held_at(place)
            for link in (1, 2):
                arrival(target(a).at[link - 1, pl.ds(0, n)], a, link - 1).wait_recv()
            for out in (1, 2):
                offset, n = across_part(place ^ 3, 3 - out)
                if n:
                    arrival(target(a).at[2, pl.ds(offset, n)], a, 3 + out).wait_recv()
            for link in (1, 2):
                direct(a, link).wait_send()
            for link in sends(a):
                hop(a, link).wait_send()
            for link in relays(a):
                forward(a, link).wait_send()

        barrier = pltpu.get_barrier_semaphore()
        for link in (1, 2):
            pl.semaphore_signal(barrier, inc=1, device_id=peer(link), device_id_type=MESH)

        @pl.when(has_next)
        def _():
            pl.semaphore_signal(barrier, inc=1, device_id={"section": section + 1}, device_id_type=MESH)

        @pl.when(has_prev)
        def _():
            pl.semaphore_signal(barrier, inc=1, device_id={"section": section - 1}, device_id_type=MESH)

        pl.semaphore_wait(barrier, 2 + has_prev.astype(jnp.int32) + has_next.astype(jnp.int32))

        @pl.when(has_next)
        def _():
            for half in range(2):
                move(half).start()

        for a in range(2):
            start(a)
        for a in range(2):
            pass_on(a)

        @pl.when(has_prev)
        def _():
            for a in (2, 3):
                move(a - 2).wait_recv()
                start(a)
            for a in (2, 3):
                pass_on(a)

        for a in range(2):
            finish(a)

        @pl.when(has_prev)
        def _():
            for a in (2, 3):
                finish(a)

        @pl.when(has_next)
        def _():
            for half in range(2):
                move(half).wait_send()

    for place in range(4):
        pl.when(me == most ^ place)(functools.partial(role, place))


def exchange(most, sections, first, last):
    halves, count, rows, width = first.shape

    def buffer(*lead):
        return jax.ShapeDtypeStruct((*lead, rows, width), jnp.bfloat16)

    hbm = pl.BlockSpec(memory_space=pl.ANY)
    return pl.pallas_call(
        functools.partial(exchange_kernel, most, sections),
        in_specs=[hbm] * 2,
        out_specs=[hbm] * 4,
        out_shape=(buffer(2, 3, 8), buffer(2, 3, 8), buffer(2, count), buffer(4, 2, 4)),
        scratch_shapes=[
            pltpu.SemaphoreType.DMA((4, 6)),
            pltpu.SemaphoreType.DMA((4, 6)),
            pltpu.SemaphoreType.DMA((2,)),
            pltpu.SemaphoreType.DMA((2,)),
        ],
        compiler_params=pltpu.CompilerParams(collective_id=most, has_side_effects=True),
        name=f"exchange_{most}",
    )(first, last)


def gram_kernel(meta_ref, own_ref, got_ref, own_last_ref, got_last_ref, fa_ref, fg_ref, ca_ref, cg_ref):
    filled = pl.program_id(0) < meta_ref[1]
    has_prev = meta_ref[2] > 0
    contract = (((0,), (0,)), ((), ()))

    def joined(own, got, half):
        return jnp.concatenate([own[half, 0], got[half, 0, 0], got[half, 1, 0], got[half, 2, 0]], axis=0)

    for half, factor_ref, cross_ref in ((0, fa_ref, ca_ref), (1, fg_ref, cg_ref)):

        @pl.when(filled)
        def _():
            latter = joined(own_ref, got_ref, half)
            factor_ref[0, 0, 0] = lax.dot_general(latter, latter, contract, preferred_element_type=jnp.float32)

        @pl.when(filled & has_prev)
        def _():
            latter = joined(own_ref, got_ref, half)
            former = joined(own_last_ref, got_last_ref, half)
            cross_ref[0, 0, 0] = lax.dot_general(former, latter, contract, preferred_element_type=jnp.float32)

        @pl.when(jnp.logical_not(filled))
        def _():
            factor_ref[...] = jnp.zeros_like(factor_ref)

        @pl.when(jnp.logical_not(filled & has_prev))
        def _():
            cross_ref[...] = jnp.zeros_like(cross_ref)


def grams(meta, first, got_first, moved, got_last):
    slots = got_first.shape[2]
    rows, width = first.shape[2:]

    def slot_of(i, meta):
        return jnp.minimum(i, jnp.maximum(meta[1] - 1, 0))

    own = pl.BlockSpec((2, 1, rows, width), lambda i, meta: (0, meta[0] + slot_of(i, meta), 0, 0))
    got = pl.BlockSpec((2, 3, 1, rows, width), lambda i, meta: (0, 0, slot_of(i, meta), 0, 0))
    out = pl.BlockSpec((1, 1, 1, width, width), lambda i, meta: (0, 0, i, 0, 0))
    shape = jax.ShapeDtypeStruct((1, 1, slots, width, width), jnp.float32)
    return pl.pallas_call(
        gram_kernel,
        grid_spec=pltpu.PrefetchScalarGridSpec(
            num_scalar_prefetch=1, grid=(slots,), in_specs=[own, got, own, got], out_specs=[out] * 4
        ),
        out_shape=(shape,) * 4,
        compiler_params=pltpu.CompilerParams(vmem_limit_bytes=40 * 2**20),
        name="grams",
    )(meta, first, got_first, moved, got_last)


def on_square(first_acts, first_grads, last_acts, last_grads, doc_lengths, block_owner):
    blocks = block_owner.shape[0]
    sections = lax.axis_size("section")
    me = lax.axis_index("dp").astype(jnp.int32)
    position = jnp.arange(blocks, dtype=jnp.int32)
    same_owner = block_owner[:, None] == block_owner[None, :]
    slot_index = jnp.sum(jnp.where(same_owner & (position[None, :] < position[:, None]), 1, 0), axis=1)
    owned = jnp.sum(jnp.where(block_owner[None, :] == jnp.arange(4)[:, None], 1, 0), axis=1).astype(jnp.int32)
    most = jnp.sum(jnp.where(owned == 8, jnp.arange(4, dtype=jnp.int32), 0))
    wanted_place = jnp.array([0] * 8 + [1] * 4 + [2] * 4 + [3] * 4, jnp.int32)
    wanted_slot = jnp.array(list(range(8)) + list(range(4)) * 3, jnp.int32)
    fits = ((block_owner ^ most)[None, :] == wanted_place[:, None]) & (slot_index[None, :] == wanted_slot[:, None])
    order = jnp.sum(jnp.where(fits, position[None, :], 0), axis=1).astype(jnp.int32)
    place = me ^ most
    base = jnp.where(place == 0, 0, 4 + 4 * place)
    mine = jnp.sum(jnp.where(block_owner == me, 1, 0))
    meta = jnp.stack([base, mine, lax.axis_index("section")]).astype(jnp.int32)
    width = first_acts.shape[2] // blocks
    first, last = arrange(order, doc_lengths[0], (first_acts, first_grads, last_acts, last_grads), width)

    def branch(which):
        def run(meta, first, last):
            got_first, got_last, moved, _ = exchange(which, sections, first, last)
            return grams(meta, first, got_first, moved, got_last)

        return run

    return lax.switch(most, [branch(which) for which in range(4)], meta, first, last)


def shifted(block, axis, distance):
    devices = range(lax.axis_size(axis))
    route = [(i - distance, i) for i in devices if i - distance in devices]
    return lax.ppermute(block, axis, route)


def row_scale(doc_lengths, row_count, docs_all):
    doc_sizes = doc_lengths.astype(jnp.float32)
    doc_end = jnp.cumsum(doc_lengths)
    starts = doc_end - doc_lengths
    places = jnp.arange(row_count, dtype=jnp.int32)
    inside = (places[:, None] >= starts[None, :]) & (places[:, None] < doc_end[None, :])
    inverse = jnp.sum(jnp.where(inside, 1.0 / doc_sizes[None, :], jnp.float32(0.0)), axis=1)
    return jnp.sqrt(inverse / docs_all)


def slot_table(block_owner, groups, slot_count):
    blocks = block_owner.shape[0]
    position = jnp.arange(blocks, dtype=jnp.int32)
    same_owner = block_owner[:, None] == block_owner[None, :]
    earlier = position[None, :] < position[:, None]
    slot_index = jnp.sum(jnp.where(same_owner & earlier, 1, 0), axis=1).astype(jnp.int32)
    target = block_owner * slot_count + slot_index
    wanted = jnp.arange(groups * slot_count, dtype=jnp.int32)
    return jnp.where(wanted[:, None] == target[None, :], 1.0, 0.0).astype(jnp.bfloat16)


def into_slots(matrix, selector, groups, slot_count):
    row_count, widths = matrix.shape
    blocks = selector.shape[1]
    block_width = widths // blocks
    blocked = matrix.reshape(row_count, blocks, block_width)
    placed = jnp.einsum("cb,rbf->crf", selector, blocked, preferred_element_type=jnp.float32)
    return placed.astype(jnp.bfloat16).reshape(groups, slot_count, row_count, block_width)


def owner_gram(former, latter):
    return jnp.einsum("gkrf,gkrh->kfh", former, latter, preferred_element_type=jnp.float32)


def on_device(first_acts, first_grads, last_acts, last_grads, doc_lengths, block_owner):
    row_count = first_acts.shape[1]
    groups = lax.axis_size("dp")
    blocks = block_owner.shape[0]
    slot_count = 2 * blocks // groups
    row_weight = row_scale(doc_lengths[0], row_count, doc_lengths.shape[1] * groups)[:, None]

    def weighted(matrix):
        return (matrix[0].astype(jnp.float32) * row_weight).astype(jnp.bfloat16)

    own_acts = weighted(first_acts)
    own_grads = weighted(first_grads)
    tail_acts = weighted(last_acts)
    tail_grads = weighted(last_grads)
    selector = slot_table(block_owner, groups, slot_count)
    acts_in = lax.all_to_all(
        into_slots(own_acts, selector, groups, slot_count),
        "dp",
        split_axis=0,
        concat_axis=0,
        tiled=True,
    )
    grads_in = lax.all_to_all(
        into_slots(own_grads, selector, groups, slot_count),
        "dp",
        split_axis=0,
        concat_axis=0,
        tiled=True,
    )
    tail_in = lax.all_to_all(
        into_slots(tail_acts, selector, groups, slot_count),
        "dp",
        split_axis=0,
        concat_axis=0,
        tiled=True,
    )
    tail_grad_in = lax.all_to_all(
        into_slots(tail_grads, selector, groups, slot_count),
        "dp",
        split_axis=0,
        concat_axis=0,
        tiled=True,
    )
    prev_in, prev_grad_in = shifted((tail_in, tail_grad_in), "section", 1)
    first = owner_gram(acts_in, acts_in)
    second = owner_gram(grads_in, grads_in)
    third = owner_gram(prev_in, acts_in)
    fourth = owner_gram(prev_grad_in, grads_in)
    results = (first[None, None], second[None, None], third[None, None], fourth[None, None])
    return results


def solution(mesh):
    placed = (
        P("section", "dp", None),
        P("section", "dp", None),
        P("section", "dp", None),
        P("section", "dp", None),
        P("dp", None),
        P(),
    )
    return jax.shard_map(
        on_square if mesh.shape["dp"] == 4 else on_device,
        mesh=mesh,
        in_specs=placed,
        out_specs=(
            P("section", "dp", None, None, None),
            P("section", "dp", None, None, None),
            P("section", "dp", None, None, None),
            P("section", "dp", None, None, None),
        ),
        check_vma=False,
    )
```

```python
import functools

import jax
import jax.numpy as jnp
from jax import lax
from jax.experimental import pallas as pl
from jax.experimental.pallas import tpu as pltpu
from jax.sharding import PartitionSpec as P

MESH = pl.DeviceIdType.MESH
GROUPS = 4

ACROSS = {0: {1: 2, 2: 2}, 1: {1: 0, 2: 4}, 2: {1: 4, 2: 0}, 3: {1: 4, 2: 4}}


def held_at(place):
    return 8 if place == 0 else 4


def base_of(place):
    return 0 if place == 0 else 8 + 4 * (place - 1)


def across_part(place, link):
    return (0 if link == 1 else ACROSS[place][1]), ACROSS[place][link]


def arrange_kernel(
    owner_ref,
    lengths_ref,
    fa_ref,
    fg_ref,
    la_ref,
    lg_ref,
    first_ref,
    last_ref,
    meta_ref,
    weight,
    staged,
    sem,
    place_of,
    count,
):
    docs = lengths_ref.shape[0]
    blocks = owner_ref.shape[0]
    rows = fa_ref.shape[1]
    width = first_ref.shape[3]
    step = pl.program_id(0)
    steps = pl.num_programs(0)

    @pl.when(step == 0)
    def _():
        row = lax.broadcasted_iota(jnp.int32, (rows, 128), 0)
        length = jnp.ones((rows, 128), jnp.int32)
        start = jnp.int32(0)
        for d in range(docs):
            size = lengths_ref[d]
            length = jnp.where((row >= start) & (row < start + size), size, length)
            start = start + size
        weight[...] = jnp.sqrt((1.0 / length.astype(jnp.float32)) / jnp.float32(docs * GROUPS))
        for g in range(GROUPS):
            count[g] = 0
        for b in range(blocks):
            owner = owner_ref[b]
            place_of[b] = count[owner]
            count[owner] = count[owner] + 1
        most = jnp.int32(0)
        for g in range(1, GROUPS):
            most = jnp.where(count[g] == 8, jnp.int32(g), most)
        for b in range(blocks):
            place = owner_ref[b] ^ most
            place_of[b] = place_of[b] + jnp.where(place == 0, 0, 4 + 4 * place)
        me = lax.axis_index("dp")
        place = me ^ most
        meta_ref[0] = jnp.where(place == 0, 0, 4 + 4 * place)
        meta_ref[1] = count[me]
        meta_ref[2] = lax.axis_index("section")
        meta_ref[3] = most

    def outgoing(at, slot):
        copies = []
        for k in range(2):
            to = place_of[2 * at + k]
            for n, ref in enumerate((first_ref, first_ref, last_ref, last_ref)):
                copies.append(pltpu.make_async_copy(staged.at[slot, k, n], ref.at[n % 2, to], sem.at[slot, k, n]))
        return copies

    slot = lax.rem(step, 2)

    @pl.when(step >= 2)
    def _():
        for one in outgoing(step - 2, slot):
            one.wait()

    row_weight = weight[:, 0:1]
    for k in range(2):
        for n, ref in enumerate((fa_ref, fg_ref, la_ref, lg_ref)):
            block = ref[0, :, k * width : (k + 1) * width].astype(jnp.float32)
            staged[slot, k, n] = (block * row_weight).astype(jnp.bfloat16)
    for one in outgoing(step, slot):
        one.start()

    @pl.when(step == steps - 1)
    def _():
        for one in outgoing(step - 1, 1 - slot):
            one.wait()
        for one in outgoing(step, slot):
            one.wait()


def arrange(owner, lengths, arrays):
    rows = arrays[0].shape[1]
    blocks = owner.shape[0]
    width = arrays[0].shape[2] // blocks
    in_spec = pl.BlockSpec((1, rows, 2 * width), lambda i, owner, lengths: (0, 0, i))
    hbm = pl.BlockSpec(memory_space=pl.ANY)
    shape = jax.ShapeDtypeStruct((2, 8 + 4 * (GROUPS - 1), rows, width), jnp.bfloat16)
    return pl.pallas_call(
        arrange_kernel,
        grid_spec=pltpu.PrefetchScalarGridSpec(
            num_scalar_prefetch=2,
            grid=(blocks // 2,),
            in_specs=[in_spec] * 4,
            out_specs=[hbm, hbm, pl.BlockSpec(memory_space=pltpu.SMEM)],
            scratch_shapes=[
                pltpu.VMEM((rows, 128), jnp.float32),
                pltpu.VMEM((2, 2, 4, rows, width), jnp.bfloat16),
                pltpu.SemaphoreType.DMA((2, 2, 4)),
                pltpu.SMEM((blocks,), jnp.int32),
                pltpu.SMEM((GROUPS,), jnp.int32),
            ],
        ),
        out_shape=(shape, shape, jax.ShapeDtypeStruct((4,), jnp.int32)),
        compiler_params=pltpu.CompilerParams(vmem_limit_bytes=60 * 2**20),
        name="arrange",
    )(owner, lengths, *arrays)


def exchange_kernel(
    most, sections, first, last, got, moved, relay, send_sem, recv_sem, move_send, move_recv
):
    me = lax.axis_index("dp")
    section = lax.axis_index("section")
    has_prev = section > 0
    has_next = section < sections - 1

    def move(half):
        return pltpu.make_async_remote_copy(
            src_ref=last.at[half],
            dst_ref=moved.at[half],
            send_sem=move_send.at[half],
            recv_sem=move_recv.at[half],
            device_id={"section": section + 1},
            device_id_type=MESH,
        )

    def role(place):
        def peer(link):
            return {"dp": most ^ place ^ link}

        def source(a):
            return first.at[a] if a < 2 else moved.at[a - 2]

        def target(a):
            return got.at[a]

        def copy(src, dst, a, sent, received, link):
            return pltpu.make_async_remote_copy(
                src_ref=src,
                dst_ref=dst,
                send_sem=send_sem.at[a, sent],
                recv_sem=recv_sem.at[a, received],
                device_id=peer(link),
                device_id_type=MESH,
            )

        def direct(a, link):
            to = place ^ link
            n = held_at(to)
            src = source(a).at[pl.ds(base_of(to), n)]
            return copy(src, target(a).at[link - 1, pl.ds(0, n)], a, link - 1, link - 1, link)

        def hop(a, link):
            offset, n = across_part(place, link)
            src = source(a).at[pl.ds(base_of(place ^ 3) + offset, n)]
            return copy(src, relay.at[a, link - 1, pl.ds(0, n)], a, 1 + link, 1 + link, link)

        def forward(a, link):
            offset, n = across_part(place ^ link, link)
            src = relay.at[a, link - 1, pl.ds(0, n)]
            out = 3 - link
            return copy(src, target(a).at[2, pl.ds(offset, n)], a, 3 + link, 3 + out, out)

        def arrival(dst, a, received):
            return copy(dst, dst, a, received, received, 1)

        def wait_hop(a, link):
            n = across_part(place ^ link, link)[1]
            arrival(relay.at[a, link - 1, pl.ds(0, n)], a, 1 + link).wait_recv()

        def sends(a):
            return [link for link in (1, 2) if ACROSS[place][link]]

        def relays(a):
            return [link for link in (1, 2) if ACROSS[place ^ link][link]]

        def start(a):
            for link in sends(a):
                hop(a, link).start()
            for link in (1, 2):
                direct(a, link).start()

        def pass_on(a):
            for link in relays(a):
                wait_hop(a, link)
                forward(a, link).start()

        def finish(a):
            n = held_at(place)
            for link in (1, 2):
                arrival(target(a).at[link - 1, pl.ds(0, n)], a, link - 1).wait_recv()
            for out in (1, 2):
                offset, n = across_part(place ^ 3, 3 - out)
                if n:
                    arrival(target(a).at[2, pl.ds(offset, n)], a, 3 + out).wait_recv()
            for link in (1, 2):
                direct(a, link).wait_send()
            for link in sends(a):
                hop(a, link).wait_send()
            for link in relays(a):
                forward(a, link).wait_send()

        barrier = pltpu.get_barrier_semaphore()
        for link in (1, 2):
            pl.semaphore_signal(barrier, inc=1, device_id=peer(link), device_id_type=MESH)

        @pl.when(has_next)
        def _():
            pl.semaphore_signal(barrier, inc=1, device_id={"section": section + 1}, device_id_type=MESH)

        @pl.when(has_prev)
        def _():
            pl.semaphore_signal(barrier, inc=1, device_id={"section": section - 1}, device_id_type=MESH)

        pl.semaphore_wait(barrier, 2 + has_prev.astype(jnp.int32) + has_next.astype(jnp.int32))

        @pl.when(has_next)
        def _():
            for half in range(2):
                move(half).start()

        for a in range(2):
            start(a)
        for a in range(2):
            pass_on(a)

        @pl.when(has_prev)
        def _():
            for a in (2, 3):
                move(a - 2).wait_recv()
                start(a)
            for a in (2, 3):
                pass_on(a)

        for a in range(2):
            finish(a)

        @pl.when(has_prev)
        def _():
            for a in (2, 3):
                finish(a)

        @pl.when(has_next)
        def _():
            for half in range(2):
                move(half).wait_send()

    for place in range(4):
        pl.when(me == most ^ place)(functools.partial(role, place))


def exchange(most, sections, first, last):
    halves, count, rows, width = first.shape

    def buffer(*lead):
        return jax.ShapeDtypeStruct((*lead, rows, width), jnp.bfloat16)

    hbm = pl.BlockSpec(memory_space=pl.ANY)
    apart = pl.BlockSpec(memory_space=pltpu.HBM)
    return pl.pallas_call(
        functools.partial(exchange_kernel, most, sections),
        in_specs=[hbm] * 2,
        out_specs=[hbm, apart, apart],
        out_shape=(buffer(4, 3, 8), buffer(2, count), buffer(4, 2, 4)),
        scratch_shapes=[
            pltpu.SemaphoreType.DMA((4, 6)),
            pltpu.SemaphoreType.DMA((4, 6)),
            pltpu.SemaphoreType.DMA((2,)),
            pltpu.SemaphoreType.DMA((2,)),
        ],
        compiler_params=pltpu.CompilerParams(collective_id=most, has_side_effects=True, vmem_limit_bytes=60 * 2**20),
        name=f"exchange_{most}",
    )(first, last)


def gram_kernel(meta_ref, own_ref, own_last_ref, got_ref, fa_ref, fg_ref, ca_ref, cg_ref):
    filled = pl.program_id(0) < meta_ref[1]
    has_prev = meta_ref[2] > 0
    contract = (((0,), (0,)), ((), ()))

    def joined(own, half, a):
        return jnp.concatenate([own[half, 0], got_ref[a, 0, 0], got_ref[a, 1, 0], got_ref[a, 2, 0]], axis=0)

    for half, factor_ref, cross_ref in ((0, fa_ref, ca_ref), (1, fg_ref, cg_ref)):

        @pl.when(filled)
        def _():
            latter = joined(own_ref, half, half)
            factor_ref[0, 0, 0] = lax.dot_general(latter, latter, contract, preferred_element_type=jnp.float32)

        @pl.when(filled & has_prev)
        def _():
            latter = joined(own_ref, half, half)
            former = joined(own_last_ref, half, 2 + half)
            cross_ref[0, 0, 0] = lax.dot_general(former, latter, contract, preferred_element_type=jnp.float32)

        @pl.when(jnp.logical_not(filled))
        def _():
            factor_ref[...] = jnp.zeros_like(factor_ref)

        @pl.when(jnp.logical_not(filled & has_prev))
        def _():
            cross_ref[...] = jnp.zeros_like(cross_ref)


def grams(meta, first, moved, got):
    slots = got.shape[2]
    rows, width = first.shape[2:]

    def slot_of(i, meta):
        return jnp.minimum(i, jnp.maximum(meta[1] - 1, 0))

    own = pl.BlockSpec((2, 1, rows, width), lambda i, meta: (0, meta[0] + slot_of(i, meta), 0, 0))
    arrived = pl.BlockSpec((4, 3, 1, rows, width), lambda i, meta: (0, 0, slot_of(i, meta), 0, 0))
    out = pl.BlockSpec((1, 1, 1, width, width), lambda i, meta: (0, 0, i, 0, 0))
    shape = jax.ShapeDtypeStruct((1, 1, slots, width, width), jnp.float32)
    return pl.pallas_call(
        gram_kernel,
        grid_spec=pltpu.PrefetchScalarGridSpec(
            num_scalar_prefetch=1, grid=(slots,), in_specs=[own, own, arrived], out_specs=[out] * 4
        ),
        out_shape=(shape,) * 4,
        compiler_params=pltpu.CompilerParams(vmem_limit_bytes=60 * 2**20),
        name="grams",
    )(meta, first, moved, got)


def on_square(first_acts, first_grads, last_acts, last_grads, doc_lengths, block_owner):
    sections = lax.axis_size("section")
    arrays = (first_acts, first_grads, last_acts, last_grads)
    first, last, meta = arrange(block_owner, doc_lengths[0], arrays)

    def branch(which):
        def run(meta, first, last):
            got, moved, _ = exchange(which, sections, first, last)
            return grams(meta, first, moved, got)

        return run

    return lax.switch(meta[3], [branch(which) for which in range(GROUPS)], meta, first, last)


def shifted(block, axis, distance):
    devices = range(lax.axis_size(axis))
    route = [(i - distance, i) for i in devices if i - distance in devices]
    return lax.ppermute(block, axis, route)


def row_scale(doc_lengths, row_count, docs_all):
    doc_sizes = doc_lengths.astype(jnp.float32)
    doc_end = jnp.cumsum(doc_lengths)
    starts = doc_end - doc_lengths
    places = jnp.arange(row_count, dtype=jnp.int32)
    inside = (places[:, None] >= starts[None, :]) & (places[:, None] < doc_end[None, :])
    inverse = jnp.sum(jnp.where(inside, 1.0 / doc_sizes[None, :], jnp.float32(0.0)), axis=1)
    return jnp.sqrt(inverse / docs_all)


def slot_table(block_owner, groups, slot_count):
    blocks = block_owner.shape[0]
    position = jnp.arange(blocks, dtype=jnp.int32)
    same_owner = block_owner[:, None] == block_owner[None, :]
    earlier = position[None, :] < position[:, None]
    slot_index = jnp.sum(jnp.where(same_owner & earlier, 1, 0), axis=1).astype(jnp.int32)
    target = block_owner * slot_count + slot_index
    wanted = jnp.arange(groups * slot_count, dtype=jnp.int32)
    return jnp.where(wanted[:, None] == target[None, :], 1.0, 0.0).astype(jnp.bfloat16)


def into_slots(matrix, selector, groups, slot_count):
    row_count, widths = matrix.shape
    blocks = selector.shape[1]
    block_width = widths // blocks
    blocked = matrix.reshape(row_count, blocks, block_width)
    placed = jnp.einsum("cb,rbf->crf", selector, blocked, preferred_element_type=jnp.float32)
    return placed.astype(jnp.bfloat16).reshape(groups, slot_count, row_count, block_width)


def owner_gram(former, latter):
    return jnp.einsum("gkrf,gkrh->kfh", former, latter, preferred_element_type=jnp.float32)


def on_device(first_acts, first_grads, last_acts, last_grads, doc_lengths, block_owner):
    row_count = first_acts.shape[1]
    groups = lax.axis_size("dp")
    blocks = block_owner.shape[0]
    slot_count = 2 * blocks // groups
    row_weight = row_scale(doc_lengths[0], row_count, doc_lengths.shape[1] * groups)[:, None]

    def weighted(matrix):
        return (matrix[0].astype(jnp.float32) * row_weight).astype(jnp.bfloat16)

    own_acts = weighted(first_acts)
    own_grads = weighted(first_grads)
    tail_acts = weighted(last_acts)
    tail_grads = weighted(last_grads)
    selector = slot_table(block_owner, groups, slot_count)
    acts_in = lax.all_to_all(
        into_slots(own_acts, selector, groups, slot_count),
        "dp",
        split_axis=0,
        concat_axis=0,
        tiled=True,
    )
    grads_in = lax.all_to_all(
        into_slots(own_grads, selector, groups, slot_count),
        "dp",
        split_axis=0,
        concat_axis=0,
        tiled=True,
    )
    tail_in = lax.all_to_all(
        into_slots(tail_acts, selector, groups, slot_count),
        "dp",
        split_axis=0,
        concat_axis=0,
        tiled=True,
    )
    tail_grad_in = lax.all_to_all(
        into_slots(tail_grads, selector, groups, slot_count),
        "dp",
        split_axis=0,
        concat_axis=0,
        tiled=True,
    )
    prev_in, prev_grad_in = shifted((tail_in, tail_grad_in), "section", 1)
    first = owner_gram(acts_in, acts_in)
    second = owner_gram(grads_in, grads_in)
    third = owner_gram(prev_in, acts_in)
    fourth = owner_gram(prev_grad_in, grads_in)
    results = (first[None, None], second[None, None], third[None, None], fourth[None, None])
    return results


def solution(mesh):
    placed = (
        P("section", "dp", None),
        P("section", "dp", None),
        P("section", "dp", None),
        P("section", "dp", None),
        P("dp", None),
        P(),
    )
    return jax.shard_map(
        on_square if mesh.shape["dp"] == GROUPS else on_device,
        mesh=mesh,
        in_specs=placed,
        out_specs=(
            P("section", "dp", None, None, None),
            P("section", "dp", None, None, None),
            P("section", "dp", None, None, None),
            P("section", "dp", None, None, None),
        ),
        check_vma=False,
    )
```

```python
import functools

import jax
import jax.numpy as jnp
from jax import lax
from jax.experimental import pallas as pl
from jax.experimental.pallas import tpu as pltpu
from jax.sharding import PartitionSpec as P

MESH = pl.DeviceIdType.MESH
GROUPS = 4

ACROSS = {0: {1: 2, 2: 2}, 1: {1: 0, 2: 4}, 2: {1: 4, 2: 0}, 3: {1: 4, 2: 4}}
ACROSS_QUARTER = {0: {1: 1, 2: 0}, 1: {1: 0, 2: 1}, 2: {1: 1, 2: 0}, 3: {1: 1, 2: 1}}
QUARTERS = 4


def held_at(place):
    return 8 if place == 0 else 4


def base_of(place):
    return 0 if place == 0 else 8 + 4 * (place - 1)


def arrange_kernel(
    owner_ref,
    lengths_ref,
    fa_ref,
    fg_ref,
    la_ref,
    lg_ref,
    first_ref,
    last_ref,
    meta_ref,
    weight,
    staged,
    sem,
    place_of,
    count,
):
    docs = lengths_ref.shape[0]
    blocks = owner_ref.shape[0]
    rows = fa_ref.shape[1]
    width = first_ref.shape[3]
    step = pl.program_id(0)
    steps = pl.num_programs(0)

    @pl.when(step == 0)
    def _():
        row = lax.broadcasted_iota(jnp.int32, (rows, 128), 0)
        length = jnp.ones((rows, 128), jnp.int32)
        start = jnp.int32(0)
        for d in range(docs):
            size = lengths_ref[d]
            length = jnp.where((row >= start) & (row < start + size), size, length)
            start = start + size
        weight[...] = jnp.sqrt((1.0 / length.astype(jnp.float32)) / jnp.float32(docs * GROUPS))
        for g in range(GROUPS):
            count[g] = 0
        for b in range(blocks):
            owner = owner_ref[b]
            place_of[b] = count[owner]
            count[owner] = count[owner] + 1
        most = jnp.int32(0)
        for g in range(1, GROUPS):
            most = jnp.where(count[g] == 8, jnp.int32(g), most)
        for b in range(blocks):
            place = owner_ref[b] ^ most
            place_of[b] = place_of[b] + jnp.where(place == 0, 0, 4 + 4 * place)
        me = lax.axis_index("dp")
        place = me ^ most
        meta_ref[0] = jnp.where(place == 0, 0, 4 + 4 * place)
        meta_ref[1] = count[me]
        meta_ref[2] = lax.axis_index("section")
        meta_ref[3] = most

    def outgoing(at, slot):
        copies = []
        for k in range(2):
            to = place_of[2 * at + k]
            for n, ref in enumerate((first_ref, first_ref, last_ref, last_ref)):
                copies.append(pltpu.make_async_copy(staged.at[slot, k, n], ref.at[n % 2, to], sem.at[slot, k, n]))
        return copies

    slot = lax.rem(step, 2)

    @pl.when(step >= 2)
    def _():
        for one in outgoing(step - 2, slot):
            one.wait()

    row_weight = jnp.concatenate([weight[...]] * (width // 128), axis=1)
    for k in range(2):
        for n, ref in enumerate((fa_ref, fg_ref, la_ref, lg_ref)):
            block = ref[0, :, k * width : (k + 1) * width].astype(jnp.float32)
            staged[slot, k, n] = (block * row_weight).astype(jnp.bfloat16)
    for one in outgoing(step, slot):
        one.start()

    @pl.when(step == steps - 1)
    def _():
        for one in outgoing(step - 1, 1 - slot):
            one.wait()
        for one in outgoing(step, slot):
            one.wait()


def arrange(owner, lengths, arrays):
    rows = arrays[0].shape[1]
    blocks = owner.shape[0]
    width = arrays[0].shape[2] // blocks
    in_spec = pl.BlockSpec((1, rows, 2 * width), lambda i, owner, lengths: (0, 0, i))
    hbm = pl.BlockSpec(memory_space=pl.ANY)
    shape = jax.ShapeDtypeStruct((2, 8 + 4 * (GROUPS - 1), rows, width), jnp.bfloat16)
    return pl.pallas_call(
        arrange_kernel,
        grid_spec=pltpu.PrefetchScalarGridSpec(
            num_scalar_prefetch=2,
            grid=(blocks // 2,),
            in_specs=[in_spec] * 4,
            out_specs=[hbm, hbm, pl.BlockSpec(memory_space=pltpu.SMEM)],
            scratch_shapes=[
                pltpu.VMEM((rows, 128), jnp.float32),
                pltpu.VMEM((2, 2, 4, rows, width), jnp.bfloat16),
                pltpu.SemaphoreType.DMA((2, 2, 4)),
                pltpu.SMEM((blocks,), jnp.int32),
                pltpu.SMEM((GROUPS,), jnp.int32),
            ],
        ),
        out_shape=(shape, shape, jax.ShapeDtypeStruct((4,), jnp.int32)),
        compiler_params=pltpu.CompilerParams(vmem_limit_bytes=60 * 2**20),
        name="arrange",
    )(owner, lengths, *arrays)


def exchange_kernel(
    most,
    sections,
    first,
    last,
    got,
    moved,
    early,
    relay,
    relay_quarter,
    send_sem,
    recv_sem,
    move_send,
    move_recv,
    on_send,
    on_recv,
):
    me = lax.axis_index("dp")
    section = lax.axis_index("section")
    plane = section // 2
    core = section - 2 * plane
    has_prev = section > 0
    has_next = section < sections - 1
    planes = sections // 2
    leaving = jnp.where(core == 1, planes - 1 - plane, 0)
    entering = jnp.where((core == 0) & has_prev, planes - plane, 0)

    def move(half):
        return pltpu.make_async_remote_copy(
            src_ref=last.at[half],
            dst_ref=moved.at[half],
            send_sem=move_send.at[half],
            recv_sem=move_recv.at[half],
            device_id={"section": section + 1},
            device_id_type=MESH,
        )

    def role(place):
        def peer(link):
            return {"dp": most ^ place ^ link}

        def go_on(half, quarter):
            m = held_at(place) // QUARTERS
            span = pl.ds(quarter * m, m)
            at = half * QUARTERS + quarter
            return pltpu.make_async_remote_copy(
                src_ref=early.at[half, :, span],
                dst_ref=got.at[2 + half, :, span],
                send_sem=on_send.at[at],
                recv_sem=on_recv.at[at],
                device_id={"section": section + 1},
                device_id_type=MESH,
            )

        class Part:
            def __init__(self, source, target, sem, relay_ref, quarter=None):
                self.source, self.target, self.sem, self.relay = source, target, sem, relay_ref
                self.quarter = quarter
                self.across = ACROSS if quarter is None else ACROSS_QUARTER
                self.sends = [link for link in (1, 2) if self.across[place][link]]
                self.relays = [link for link in (1, 2) if self.across[place ^ link][link]]

            def span(self, to, offset, n, base=0):
                if self.quarter is not None:
                    offset = offset + self.quarter * (held_at(to) // QUARTERS)
                return pl.ds(base + offset, n)

            def size(self, to):
                return held_at(to) if self.quarter is None else held_at(to) // QUARTERS

            def part(self, source_place, link):
                return (0 if link == 1 else self.across[source_place][1]), self.across[source_place][link]

            def copy(self, src, dst, sent, received, link):
                return pltpu.make_async_remote_copy(
                    src_ref=src,
                    dst_ref=dst,
                    send_sem=send_sem.at[self.sem, sent],
                    recv_sem=recv_sem.at[self.sem, received],
                    device_id=peer(link),
                    device_id_type=MESH,
                )

            def direct(self, link):
                to = place ^ link
                n = self.size(to)
                src = self.source.at[self.span(to, 0, n, base_of(to))]
                return self.copy(src, self.target.at[link - 1, self.span(to, 0, n)], link - 1, link - 1, link)

            def hop(self, link):
                offset, n = self.part(place, link)
                to = place ^ 3
                src = self.source.at[self.span(to, offset, n, base_of(to))]
                return self.copy(src, self.relay.at[link - 1, pl.ds(0, n)], 1 + link, 1 + link, link)

            def forward(self, link):
                offset, n = self.part(place ^ link, link)
                out = 3 - link
                to = place ^ out
                dst = self.target.at[2, self.span(to, offset, n)]
                return self.copy(self.relay.at[link - 1, pl.ds(0, n)], dst, 3 + link, 3 + out, out)

            def arrival(self, dst, received):
                return self.copy(dst, dst, received, received, 1)

            def start(self):
                for link in self.sends:
                    self.hop(link).start()
                for link in (1, 2):
                    self.direct(link).start()

            def pass_on(self):
                for link in self.relays:
                    n = self.part(place ^ link, link)[1]
                    self.arrival(self.relay.at[link - 1, pl.ds(0, n)], 1 + link).wait_recv()
                    self.forward(link).start()

            def wait_arrivals(self):
                n = self.size(place)
                for link in (1, 2):
                    self.arrival(self.target.at[link - 1, self.span(place, 0, n)], link - 1).wait_recv()
                for out in (1, 2):
                    offset, n = self.part(place ^ 3, 3 - out)
                    if n:
                        self.arrival(self.target.at[2, self.span(place, offset, n)], 3 + out).wait_recv()

            def wait_sent(self):
                for link in (1, 2):
                    self.direct(link).wait_send()
                for link in self.sends:
                    self.hop(link).wait_send()
                for link in self.relays:
                    self.forward(link).wait_send()

        def whole(half):
            return Part(first.at[half], got.at[half], half, relay.at[half])

        def late(half, quarter):
            at = half * QUARTERS + quarter
            return Part(moved.at[half], got.at[2 + half], 2 + at, relay_quarter.at[at], quarter)

        def ahead(half, quarter):
            at = (2 + half) * QUARTERS + quarter
            return Part(last.at[half], early.at[half], 2 + at, relay_quarter.at[at], quarter)

        def each(low, high, act):
            for half in range(2):

                @pl.loop(low, high)
                def _(quarter):
                    act(half, quarter)

        barrier = pltpu.get_barrier_semaphore()
        for link in (1, 2):
            pl.semaphore_signal(barrier, inc=1, device_id=peer(link), device_id_type=MESH)

        @pl.when(has_next)
        def _():
            pl.semaphore_signal(barrier, inc=1, device_id={"section": section + 1}, device_id_type=MESH)

        @pl.when(has_prev)
        def _():
            pl.semaphore_signal(barrier, inc=1, device_id={"section": section - 1}, device_id_type=MESH)

        pl.semaphore_wait(barrier, 2 + has_prev.astype(jnp.int32) + has_next.astype(jnp.int32))

        @pl.when(has_next)
        def _():
            for half in range(2):
                move(half).start()

        for half in range(2):
            whole(half).start()
        each(0, leaving, lambda half, quarter: ahead(half, quarter).start())
        for half in range(2):
            whole(half).pass_on()
        each(0, leaving, lambda half, quarter: ahead(half, quarter).pass_on())

        late_from = jnp.where(has_prev, entering, QUARTERS)

        @pl.when(has_prev)
        def _():
            for half in range(2):
                move(half).wait_recv()

        each(late_from, QUARTERS, lambda half, quarter: late(half, quarter).start())

        def send_on(half, quarter):
            ahead(half, quarter).wait_arrivals()
            go_on(half, quarter).start()

        each(0, leaving, send_on)
        each(late_from, QUARTERS, lambda half, quarter: late(half, quarter).pass_on())

        for half in range(2):
            whole(half).wait_arrivals()
        each(late_from, QUARTERS, lambda half, quarter: late(half, quarter).wait_arrivals())
        each(0, entering, lambda half, quarter: go_on(half, quarter).wait_recv())
        for half in range(2):
            whole(half).wait_sent()
        each(0, leaving, lambda half, quarter: ahead(half, quarter).wait_sent())
        each(0, leaving, lambda half, quarter: go_on(half, quarter).wait_send())
        each(late_from, QUARTERS, lambda half, quarter: late(half, quarter).wait_sent())

        @pl.when(has_next)
        def _():
            for half in range(2):
                move(half).wait_send()

    for place in range(4):
        pl.when(me == most ^ place)(functools.partial(role, place))


def exchange(most, sections, first, last):
    halves, count, rows, width = first.shape

    def buffer(*lead):
        return jax.ShapeDtypeStruct((*lead, rows, width), jnp.bfloat16)

    hbm = pl.BlockSpec(memory_space=pl.ANY)
    return pl.pallas_call(
        functools.partial(exchange_kernel, most, sections),
        in_specs=[hbm] * 2,
        out_specs=[hbm] * 5,
        out_shape=(
            buffer(4, 3, 8),
            buffer(2, count),
            buffer(2, 3, 8),
            buffer(2, 2, 4),
            buffer(4 * QUARTERS, 2, 1),
        ),
        scratch_shapes=[
            pltpu.SemaphoreType.DMA((2 + 4 * QUARTERS, 6)),
            pltpu.SemaphoreType.DMA((2 + 4 * QUARTERS, 6)),
            pltpu.SemaphoreType.DMA((2,)),
            pltpu.SemaphoreType.DMA((2,)),
            pltpu.SemaphoreType.DMA((2 * QUARTERS,)),
            pltpu.SemaphoreType.DMA((2 * QUARTERS,)),
        ],
        compiler_params=pltpu.CompilerParams(
            collective_id=most, has_side_effects=True, vmem_limit_bytes=60 * 2**20
        ),
        name=f"exchange_{most}",
    )(first, last)


def gram_kernel(meta_ref, own_ref, own_last_ref, got_ref, got_last_ref, fa_ref, fg_ref, ca_ref, cg_ref):
    side = pl.program_id(0)
    filled = pl.program_id(1) < meta_ref[1]
    crossed = filled & (meta_ref[2] > 0)
    contract = (((0,), (0,)), ((), ()))

    def joined(own, got):
        return jnp.concatenate([own[0, 0], got[0, 0, 0], got[0, 1, 0], got[0, 2, 0]], axis=0)

    for half, factor_ref, cross_ref in ((0, fa_ref, ca_ref), (1, fg_ref, cg_ref)):

        @pl.when((side == half) & filled)
        def _():
            latter = joined(own_ref, got_ref)
            factor_ref[0, 0, 0] = lax.dot_general(latter, latter, contract, preferred_element_type=jnp.float32)

        @pl.when((side == half) & crossed)
        def _():
            latter = joined(own_ref, got_ref)
            former = joined(own_last_ref, got_last_ref)
            cross_ref[0, 0, 0] = lax.dot_general(former, latter, contract, preferred_element_type=jnp.float32)

        @pl.when((side == half) & jnp.logical_not(filled))
        def _():
            factor_ref[...] = jnp.zeros_like(factor_ref)

        @pl.when((side == half) & jnp.logical_not(crossed))
        def _():
            cross_ref[...] = jnp.zeros_like(cross_ref)


def grams(meta, first, moved, got):
    slots = got.shape[2]
    rows, width = first.shape[2:]

    def slot_of(i, meta):
        return jnp.minimum(i, jnp.maximum(meta[1] - 1, 0))

    def arrived(skip):
        return pl.BlockSpec((1, 3, 1, rows, width), lambda h, i, meta: (skip + h, 0, slot_of(i, meta), 0, 0))

    own = pl.BlockSpec((1, 1, rows, width), lambda h, i, meta: (h, meta[0] + slot_of(i, meta), 0, 0))
    block = (1, 1, 1, width, width)
    acts = pl.BlockSpec(block, lambda h, i, meta: (0, 0, jnp.where(h == 0, i, slots - 1), 0, 0))
    grads = pl.BlockSpec(block, lambda h, i, meta: (0, 0, jnp.where(h == 0, 0, i), 0, 0))
    shape = jax.ShapeDtypeStruct((1, 1, slots, width, width), jnp.float32)
    return pl.pallas_call(
        gram_kernel,
        grid_spec=pltpu.PrefetchScalarGridSpec(
            num_scalar_prefetch=1,
            grid=(2, slots),
            in_specs=[own, own, arrived(0), arrived(2)],
            out_specs=[acts, grads, acts, grads],
        ),
        out_shape=(shape,) * 4,
        compiler_params=pltpu.CompilerParams(vmem_limit_bytes=60 * 2**20),
        name="grams",
    )(meta, first, moved, got, got)


def on_square(first_acts, first_grads, last_acts, last_grads, doc_lengths, block_owner):
    sections = lax.axis_size("section")
    arrays = (first_acts, first_grads, last_acts, last_grads)
    first, last, meta = arrange(block_owner, doc_lengths[0], arrays)

    def branch(which):
        def run(meta, first, last):
            got, moved, *_ = exchange(which, sections, first, last)
            return grams(meta, first, moved, got)

        return run

    return lax.switch(meta[3], [branch(which) for which in range(GROUPS)], meta, first, last)


def shifted(block, axis, distance):
    devices = range(lax.axis_size(axis))
    route = [(i - distance, i) for i in devices if i - distance in devices]
    return lax.ppermute(block, axis, route)


def row_scale(doc_lengths, row_count, docs_all):
    doc_sizes = doc_lengths.astype(jnp.float32)
    doc_end = jnp.cumsum(doc_lengths)
    starts = doc_end - doc_lengths
    places = jnp.arange(row_count, dtype=jnp.int32)
    inside = (places[:, None] >= starts[None, :]) & (places[:, None] < doc_end[None, :])
    inverse = jnp.sum(jnp.where(inside, 1.0 / doc_sizes[None, :], jnp.float32(0.0)), axis=1)
    return jnp.sqrt(inverse / docs_all)


def slot_table(block_owner, groups, slot_count):
    blocks = block_owner.shape[0]
    position = jnp.arange(blocks, dtype=jnp.int32)
    same_owner = block_owner[:, None] == block_owner[None, :]
    earlier = position[None, :] < position[:, None]
    slot_index = jnp.sum(jnp.where(same_owner & earlier, 1, 0), axis=1).astype(jnp.int32)
    target = block_owner * slot_count + slot_index
    wanted = jnp.arange(groups * slot_count, dtype=jnp.int32)
    return jnp.where(wanted[:, None] == target[None, :], 1.0, 0.0).astype(jnp.bfloat16)


def into_slots(matrix, selector, groups, slot_count):
    row_count, widths = matrix.shape
    blocks = selector.shape[1]
    block_width = widths // blocks
    blocked = matrix.reshape(row_count, blocks, block_width)
    placed = jnp.einsum("cb,rbf->crf", selector, blocked, preferred_element_type=jnp.float32)
    return placed.astype(jnp.bfloat16).reshape(groups, slot_count, row_count, block_width)


def owner_gram(former, latter):
    return jnp.einsum("gkrf,gkrh->kfh", former, latter, preferred_element_type=jnp.float32)


def on_device(first_acts, first_grads, last_acts, last_grads, doc_lengths, block_owner):
    row_count = first_acts.shape[1]
    groups = lax.axis_size("dp")
    blocks = block_owner.shape[0]
    slot_count = 2 * blocks // groups
    row_weight = row_scale(doc_lengths[0], row_count, doc_lengths.shape[1] * groups)[:, None]

    def weighted(matrix):
        return (matrix[0].astype(jnp.float32) * row_weight).astype(jnp.bfloat16)

    own_acts = weighted(first_acts)
    own_grads = weighted(first_grads)
    tail_acts = weighted(last_acts)
    tail_grads = weighted(last_grads)
    selector = slot_table(block_owner, groups, slot_count)
    acts_in = lax.all_to_all(
        into_slots(own_acts, selector, groups, slot_count),
        "dp",
        split_axis=0,
        concat_axis=0,
        tiled=True,
    )
    grads_in = lax.all_to_all(
        into_slots(own_grads, selector, groups, slot_count),
        "dp",
        split_axis=0,
        concat_axis=0,
        tiled=True,
    )
    tail_in = lax.all_to_all(
        into_slots(tail_acts, selector, groups, slot_count),
        "dp",
        split_axis=0,
        concat_axis=0,
        tiled=True,
    )
    tail_grad_in = lax.all_to_all(
        into_slots(tail_grads, selector, groups, slot_count),
        "dp",
        split_axis=0,
        concat_axis=0,
        tiled=True,
    )
    prev_in, prev_grad_in = shifted((tail_in, tail_grad_in), "section", 1)
    first = owner_gram(acts_in, acts_in)
    second = owner_gram(grads_in, grads_in)
    third = owner_gram(prev_in, acts_in)
    fourth = owner_gram(prev_grad_in, grads_in)
    results = (first[None, None], second[None, None], third[None, None], fourth[None, None])
    return results


def solution(mesh):
    placed = (
        P("section", "dp", None),
        P("section", "dp", None),
        P("section", "dp", None),
        P("section", "dp", None),
        P("dp", None),
        P(),
    )
    return jax.shard_map(
        on_square if mesh.shape["dp"] == GROUPS else on_device,
        mesh=mesh,
        in_specs=placed,
        out_specs=(
            P("section", "dp", None, None, None),
            P("section", "dp", None, None, None),
            P("section", "dp", None, None, None),
            P("section", "dp", None, None, None),
        ),
        check_vma=False,
    )
```

```python
import functools

import jax
import jax.numpy as jnp
from jax import lax
from jax.experimental import pallas as pl
from jax.experimental.pallas import tpu as pltpu
from jax.sharding import PartitionSpec as P

MESH = pl.DeviceIdType.MESH
GROUPS = 4

ACROSS = {0: {1: 2, 2: 2}, 1: {1: 0, 2: 4}, 2: {1: 4, 2: 0}, 3: {1: 4, 2: 4}}
ACROSS_QUARTER = {0: {1: 1, 2: 0}, 1: {1: 0, 2: 1}, 2: {1: 1, 2: 0}, 3: {1: 1, 2: 1}}
QUARTERS = 4


def held_at(place):
    return 8 if place == 0 else 4


def base_of(place):
    return 0 if place == 0 else 8 + 4 * (place - 1)


def arrange_kernel(
    owner_ref,
    lengths_ref,
    fa_ref,
    fg_ref,
    la_ref,
    lg_ref,
    first_ref,
    last_ref,
    meta_ref,
    weight,
    held,
    read_sem,
    write_sem,
    place_of,
    count,
):
    docs = lengths_ref.shape[0]
    blocks, _, rows, width = held.shape

    def read(b, n):
        ref = (fa_ref, fg_ref, la_ref, lg_ref)[n]
        span = pl.ds(pl.multiple_of(b * width, width), width)
        return pltpu.make_async_copy(ref.at[0, :, span], held.at[b, n], read_sem.at[b, n])

    def write(b, n):
        ref = (first_ref, first_ref, last_ref, last_ref)[n]
        return pltpu.make_async_copy(held.at[b, n], ref.at[n % 2, place_of[b]], write_sem.at[b, n])

    @pl.loop(0, blocks)
    def _(b):
        for n in range(4):
            read(b, n).start()

    row = lax.broadcasted_iota(jnp.int32, (rows, 128), 0)
    length = jnp.ones((rows, 128), jnp.int32)
    start = jnp.int32(0)
    for d in range(docs):
        size = lengths_ref[d]
        length = jnp.where((row >= start) & (row < start + size), size, length)
        start = start + size
    weight[...] = jnp.sqrt((1.0 / length.astype(jnp.float32)) / jnp.float32(docs * GROUPS))
    for g in range(GROUPS):
        count[g] = 0
    for b in range(blocks):
        owner = owner_ref[b]
        place_of[b] = count[owner]
        count[owner] = count[owner] + 1
    most = jnp.int32(0)
    for g in range(1, GROUPS):
        most = jnp.where(count[g] == 8, jnp.int32(g), most)
    for b in range(blocks):
        place = owner_ref[b] ^ most
        place_of[b] = place_of[b] + jnp.where(place == 0, 0, 4 + 4 * place)
    me = lax.axis_index("dp")
    place = me ^ most
    meta_ref[0] = jnp.where(place == 0, 0, 4 + 4 * place)
    meta_ref[1] = count[me]
    meta_ref[2] = lax.axis_index("section")
    meta_ref[3] = most

    @pl.loop(0, blocks)
    def _(b):
        row_weight = jnp.concatenate([weight[...]] * (width // 128), axis=1)
        for n in range(4):
            read(b, n).wait()
            held[b, n] = (held[b, n].astype(jnp.float32) * row_weight).astype(jnp.bfloat16)
            write(b, n).start()

    @pl.loop(0, blocks)
    def _(b):
        for n in range(4):
            write(b, n).wait()


def arrange(owner, lengths, arrays):
    rows = arrays[0].shape[1]
    blocks = owner.shape[0]
    width = arrays[0].shape[2] // blocks
    hbm = pl.BlockSpec(memory_space=pl.ANY)
    smem = pl.BlockSpec(memory_space=pltpu.SMEM)
    shape = jax.ShapeDtypeStruct((2, 8 + 4 * (GROUPS - 1), rows, width), jnp.bfloat16)
    return pl.pallas_call(
        arrange_kernel,
        in_specs=[smem, smem] + [hbm] * 4,
        out_specs=[hbm, hbm, smem],
        scratch_shapes=[
            pltpu.VMEM((rows, 128), jnp.float32),
            pltpu.VMEM((blocks, 4, rows, width), jnp.bfloat16),
            pltpu.SemaphoreType.DMA((blocks, 4)),
            pltpu.SemaphoreType.DMA((blocks, 4)),
            pltpu.SMEM((blocks,), jnp.int32),
            pltpu.SMEM((GROUPS,), jnp.int32),
        ],
        out_shape=(shape, shape, jax.ShapeDtypeStruct((4,), jnp.int32)),
        compiler_params=pltpu.CompilerParams(vmem_limit_bytes=60 * 2**20),
        name="arrange",
    )(owner, lengths, *arrays)


def exchange_kernel(
    most,
    sections,
    first,
    last,
    got,
    moved,
    early,
    relay,
    relay_quarter,
    send_sem,
    recv_sem,
    move_send,
    move_recv,
    on_send,
    on_recv,
):
    me = lax.axis_index("dp")
    section = lax.axis_index("section")
    plane = section // 2
    core = section - 2 * plane
    has_prev = section > 0
    has_next = section < sections - 1
    planes = sections // 2
    leaving = jnp.where(core == 1, planes - 1 - plane, 0)
    entering = jnp.where((core == 0) & has_prev, planes - plane, 0)

    def role(place):
        def peer(link):
            return {"dp": most ^ place ^ link}

        others = [at for at in range(4) if at != place]

        def move(half, at, quarter=None):
            n = held_at(at) if quarter is None else held_at(at) // QUARTERS
            span = pl.ds(base_of(at) + (0 if quarter is None else quarter * n), n)
            index = 0 if quarter is None else quarter
            return pltpu.make_async_remote_copy(
                src_ref=last.at[half, span],
                dst_ref=moved.at[half, span],
                send_sem=move_send.at[half, at, index],
                recv_sem=move_recv.at[half, at, index],
                device_id={"section": section + 1},
                device_id_type=MESH,
            )

        def go_on(half, quarter):
            m = held_at(place) // QUARTERS
            span = pl.ds(quarter * m, m)
            at = half * QUARTERS + quarter
            return pltpu.make_async_remote_copy(
                src_ref=early.at[half, :, span],
                dst_ref=got.at[2 + half, :, span],
                send_sem=on_send.at[at],
                recv_sem=on_recv.at[at],
                device_id={"section": section + 1},
                device_id_type=MESH,
            )

        class Part:
            def __init__(self, source, target, sem, relay_ref, quarter=None):
                self.source, self.target, self.sem, self.relay = source, target, sem, relay_ref
                self.quarter = quarter
                self.across = ACROSS if quarter is None else ACROSS_QUARTER
                self.sends = [link for link in (1, 2) if self.across[place][link]]
                self.relays = [link for link in (1, 2) if self.across[place ^ link][link]]

            def span(self, to, offset, n, base=0):
                if self.quarter is not None:
                    offset = offset + self.quarter * (held_at(to) // QUARTERS)
                return pl.ds(base + offset, n)

            def size(self, to):
                return held_at(to) if self.quarter is None else held_at(to) // QUARTERS

            def part(self, source_place, link):
                return (0 if link == 1 else self.across[source_place][1]), self.across[source_place][link]

            def copy(self, src, dst, sent, received, link):
                return pltpu.make_async_remote_copy(
                    src_ref=src,
                    dst_ref=dst,
                    send_sem=send_sem.at[self.sem, sent],
                    recv_sem=recv_sem.at[self.sem, received],
                    device_id=peer(link),
                    device_id_type=MESH,
                )

            def direct(self, link):
                to = place ^ link
                n = self.size(to)
                src = self.source.at[self.span(to, 0, n, base_of(to))]
                return self.copy(src, self.target.at[link - 1, self.span(to, 0, n)], link - 1, link - 1, link)

            def hop(self, link):
                offset, n = self.part(place, link)
                to = place ^ 3
                src = self.source.at[self.span(to, offset, n, base_of(to))]
                return self.copy(src, self.relay.at[link - 1, pl.ds(0, n)], 1 + link, 1 + link, link)

            def forward(self, link):
                offset, n = self.part(place ^ link, link)
                out = 3 - link
                to = place ^ out
                dst = self.target.at[2, self.span(to, offset, n)]
                return self.copy(self.relay.at[link - 1, pl.ds(0, n)], dst, 3 + link, 3 + out, out)

            def arrival(self, dst, received):
                return self.copy(dst, dst, received, received, 1)

            def start(self):
                for link in self.sends:
                    self.hop(link).start()
                for link in (1, 2):
                    self.direct(link).start()

            def pass_on(self):
                for link in self.relays:
                    n = self.part(place ^ link, link)[1]
                    self.arrival(self.relay.at[link - 1, pl.ds(0, n)], 1 + link).wait_recv()
                    self.forward(link).start()

            def wait_arrivals(self):
                n = self.size(place)
                for link in (1, 2):
                    self.arrival(self.target.at[link - 1, self.span(place, 0, n)], link - 1).wait_recv()
                for out in (1, 2):
                    offset, n = self.part(place ^ 3, 3 - out)
                    if n:
                        self.arrival(self.target.at[2, self.span(place, offset, n)], 3 + out).wait_recv()

            def wait_sent(self):
                for link in (1, 2):
                    self.direct(link).wait_send()
                for link in self.sends:
                    self.hop(link).wait_send()
                for link in self.relays:
                    self.forward(link).wait_send()

        def whole(half):
            return Part(first.at[half], got.at[half], half, relay.at[half])

        def late(half, quarter):
            at = half * QUARTERS + quarter
            return Part(moved.at[half], got.at[2 + half], 2 + at, relay_quarter.at[at], quarter)

        def ahead(half, quarter):
            at = (2 + half) * QUARTERS + quarter
            return Part(last.at[half], early.at[half], 2 + at, relay_quarter.at[at], quarter)

        def each(low, high, act):
            for half in range(2):

                @pl.loop(low, high)
                def _(quarter):
                    act(half, quarter)

        barrier = pltpu.get_barrier_semaphore()
        for link in (1, 2):
            pl.semaphore_signal(barrier, inc=1, device_id=peer(link), device_id_type=MESH)

        @pl.when(has_next)
        def _():
            pl.semaphore_signal(barrier, inc=1, device_id={"section": section + 1}, device_id_type=MESH)

        @pl.when(has_prev)
        def _():
            pl.semaphore_signal(barrier, inc=1, device_id={"section": section - 1}, device_id_type=MESH)

        pl.semaphore_wait(barrier, 2 + has_prev.astype(jnp.int32) + has_next.astype(jnp.int32))

        late_from = jnp.where(has_prev, entering, QUARTERS)
        moving_from = jnp.where(has_next, leaving, QUARTERS)

        def start_moves(half, quarter):
            for at in others:
                move(half, at, quarter).start()

        def start_late(half, quarter):
            for at in others:
                move(half, at, quarter).wait_recv()
            late(half, quarter).start()

        def send_on(half, quarter):
            ahead(half, quarter).wait_arrivals()
            go_on(half, quarter).start()

        def wait_moves(half, quarter):
            for at in others:
                move(half, at, quarter).wait_send()

        each(moving_from, QUARTERS, start_moves)
        each(0, leaving, lambda half, quarter: ahead(half, quarter).start())
        for half in range(2):
            whole(half).start()

        @pl.when(has_next)
        def _():
            for half in range(2):
                move(half, place).start()

        each(0, leaving, lambda half, quarter: ahead(half, quarter).pass_on())
        for half in range(2):
            whole(half).pass_on()
        each(late_from, QUARTERS, start_late)
        each(0, leaving, send_on)
        each(late_from, QUARTERS, lambda half, quarter: late(half, quarter).pass_on())

        for half in range(2):
            whole(half).wait_arrivals()
        each(late_from, QUARTERS, lambda half, quarter: late(half, quarter).wait_arrivals())
        each(0, entering, lambda half, quarter: go_on(half, quarter).wait_recv())

        @pl.when(has_prev)
        def _():
            for half in range(2):
                move(half, place).wait_recv()

        for half in range(2):
            whole(half).wait_sent()
        each(0, leaving, lambda half, quarter: ahead(half, quarter).wait_sent())
        each(0, leaving, lambda half, quarter: go_on(half, quarter).wait_send())
        each(late_from, QUARTERS, lambda half, quarter: late(half, quarter).wait_sent())
        each(moving_from, QUARTERS, wait_moves)

        @pl.when(has_next)
        def _():
            for half in range(2):
                move(half, place).wait_send()

    for place in range(4):
        pl.when(me == most ^ place)(functools.partial(role, place))


def exchange(most, sections, first, last):
    halves, count, rows, width = first.shape

    def buffer(*lead):
        return jax.ShapeDtypeStruct((*lead, rows, width), jnp.bfloat16)

    hbm = pl.BlockSpec(memory_space=pl.ANY)
    return pl.pallas_call(
        functools.partial(exchange_kernel, most, sections),
        in_specs=[hbm] * 2,
        out_specs=[hbm] * 5,
        out_shape=(
            buffer(4, 3, 8),
            buffer(2, count),
            buffer(2, 3, 8),
            buffer(2, 2, 4),
            buffer(4 * QUARTERS, 2, 1),
        ),
        scratch_shapes=[
            pltpu.SemaphoreType.DMA((2 + 4 * QUARTERS, 6)),
            pltpu.SemaphoreType.DMA((2 + 4 * QUARTERS, 6)),
            pltpu.SemaphoreType.DMA((2, 4, QUARTERS)),
            pltpu.SemaphoreType.DMA((2, 4, QUARTERS)),
            pltpu.SemaphoreType.DMA((2 * QUARTERS,)),
            pltpu.SemaphoreType.DMA((2 * QUARTERS,)),
        ],
        compiler_params=pltpu.CompilerParams(
            collective_id=most, has_side_effects=True, vmem_limit_bytes=60 * 2**20
        ),
        name=f"exchange_{most}",
    )(first, last)


def gram_kernel(meta_ref, own_ref, own_last_ref, got_ref, fa_ref, fg_ref, ca_ref, cg_ref):
    filled = pl.program_id(0) < meta_ref[1]
    has_prev = meta_ref[2] > 0
    contract = (((0,), (0,)), ((), ()))

    def joined(own, half, a):
        return jnp.concatenate([own[half, 0], got_ref[a, 0, 0], got_ref[a, 1, 0], got_ref[a, 2, 0]], axis=0)

    for half, factor_ref, cross_ref in ((0, fa_ref, ca_ref), (1, fg_ref, cg_ref)):

        @pl.when(filled & jnp.logical_not(has_prev))
        def _():
            latter = joined(own_ref, half, half)
            factor_ref[0, 0, 0] = lax.dot_general(latter, latter, contract, preferred_element_type=jnp.float32)

        @pl.when(filled & has_prev)
        def _():
            latter = joined(own_ref, half, half)
            both = jnp.concatenate([latter, joined(own_last_ref, half, 2 + half)], axis=1)
            products = lax.dot_general(both, latter, contract, preferred_element_type=jnp.float32)
            factor_ref[0, 0, 0] = products[: latter.shape[1]]
            cross_ref[0, 0, 0] = products[latter.shape[1] :]

        @pl.when(jnp.logical_not(filled))
        def _():
            factor_ref[...] = jnp.zeros_like(factor_ref)

        @pl.when(jnp.logical_not(filled & has_prev))
        def _():
            cross_ref[...] = jnp.zeros_like(cross_ref)


def grams(meta, first, moved, got):
    slots = got.shape[2]
    rows, width = first.shape[2:]

    def slot_of(i, meta):
        return jnp.minimum(i, jnp.maximum(meta[1] - 1, 0))

    own = pl.BlockSpec((2, 1, rows, width), lambda i, meta: (0, meta[0] + slot_of(i, meta), 0, 0))
    arrived = pl.BlockSpec((4, 3, 1, rows, width), lambda i, meta: (0, 0, slot_of(i, meta), 0, 0))
    out = pl.BlockSpec((1, 1, 1, width, width), lambda i, meta: (0, 0, i, 0, 0))
    shape = jax.ShapeDtypeStruct((1, 1, slots, width, width), jnp.float32)
    return pl.pallas_call(
        gram_kernel,
        grid_spec=pltpu.PrefetchScalarGridSpec(
            num_scalar_prefetch=1, grid=(slots,), in_specs=[own, own, arrived], out_specs=[out] * 4
        ),
        out_shape=(shape,) * 4,
        compiler_params=pltpu.CompilerParams(vmem_limit_bytes=60 * 2**20),
        name="grams",
    )(meta, first, moved, got)


def on_square(first_acts, first_grads, last_acts, last_grads, doc_lengths, block_owner):
    sections = lax.axis_size("section")
    arrays = (first_acts, first_grads, last_acts, last_grads)
    first, last, meta = arrange(block_owner, doc_lengths[0], arrays)

    def branch(which):
        def run(meta, first, last):
            got, moved, *_ = exchange(which, sections, first, last)
            return grams(meta, first, moved, got)

        return run

    return lax.switch(meta[3], [branch(which) for which in range(GROUPS)], meta, first, last)


def shifted(block, axis, distance):
    devices = range(lax.axis_size(axis))
    route = [(i - distance, i) for i in devices if i - distance in devices]
    return lax.ppermute(block, axis, route)


def row_scale(doc_lengths, row_count, docs_all):
    doc_sizes = doc_lengths.astype(jnp.float32)
    doc_end = jnp.cumsum(doc_lengths)
    starts = doc_end - doc_lengths
    places = jnp.arange(row_count, dtype=jnp.int32)
    inside = (places[:, None] >= starts[None, :]) & (places[:, None] < doc_end[None, :])
    inverse = jnp.sum(jnp.where(inside, 1.0 / doc_sizes[None, :], jnp.float32(0.0)), axis=1)
    return jnp.sqrt(inverse / docs_all)


def slot_table(block_owner, groups, slot_count):
    blocks = block_owner.shape[0]
    position = jnp.arange(blocks, dtype=jnp.int32)
    same_owner = block_owner[:, None] == block_owner[None, :]
    earlier = position[None, :] < position[:, None]
    slot_index = jnp.sum(jnp.where(same_owner & earlier, 1, 0), axis=1).astype(jnp.int32)
    target = block_owner * slot_count + slot_index
    wanted = jnp.arange(groups * slot_count, dtype=jnp.int32)
    return jnp.where(wanted[:, None] == target[None, :], 1.0, 0.0).astype(jnp.bfloat16)


def into_slots(matrix, selector, groups, slot_count):
    row_count, widths = matrix.shape
    blocks = selector.shape[1]
    block_width = widths // blocks
    blocked = matrix.reshape(row_count, blocks, block_width)
    placed = jnp.einsum("cb,rbf->crf", selector, blocked, preferred_element_type=jnp.float32)
    return placed.astype(jnp.bfloat16).reshape(groups, slot_count, row_count, block_width)


def owner_gram(former, latter):
    return jnp.einsum("gkrf,gkrh->kfh", former, latter, preferred_element_type=jnp.float32)


def on_device(first_acts, first_grads, last_acts, last_grads, doc_lengths, block_owner):
    row_count = first_acts.shape[1]
    groups = lax.axis_size("dp")
    blocks = block_owner.shape[0]
    slot_count = 2 * blocks // groups
    row_weight = row_scale(doc_lengths[0], row_count, doc_lengths.shape[1] * groups)[:, None]

    def weighted(matrix):
        return (matrix[0].astype(jnp.float32) * row_weight).astype(jnp.bfloat16)

    own_acts = weighted(first_acts)
    own_grads = weighted(first_grads)
    tail_acts = weighted(last_acts)
    tail_grads = weighted(last_grads)
    selector = slot_table(block_owner, groups, slot_count)
    acts_in = lax.all_to_all(
        into_slots(own_acts, selector, groups, slot_count),
        "dp",
        split_axis=0,
        concat_axis=0,
        tiled=True,
    )
    grads_in = lax.all_to_all(
        into_slots(own_grads, selector, groups, slot_count),
        "dp",
        split_axis=0,
        concat_axis=0,
        tiled=True,
    )
    tail_in = lax.all_to_all(
        into_slots(tail_acts, selector, groups, slot_count),
        "dp",
        split_axis=0,
        concat_axis=0,
        tiled=True,
    )
    tail_grad_in = lax.all_to_all(
        into_slots(tail_grads, selector, groups, slot_count),
        "dp",
        split_axis=0,
        concat_axis=0,
        tiled=True,
    )
    prev_in, prev_grad_in = shifted((tail_in, tail_grad_in), "section", 1)
    first = owner_gram(acts_in, acts_in)
    second = owner_gram(grads_in, grads_in)
    third = owner_gram(prev_in, acts_in)
    fourth = owner_gram(prev_grad_in, grads_in)
    results = (first[None, None], second[None, None], third[None, None], fourth[None, None])
    return results


def solution(mesh):
    placed = (
        P("section", "dp", None),
        P("section", "dp", None),
        P("section", "dp", None),
        P("section", "dp", None),
        P("dp", None),
        P(),
    )
    return jax.shard_map(
        on_square if mesh.shape["dp"] == GROUPS else on_device,
        mesh=mesh,
        in_specs=placed,
        out_specs=(
            P("section", "dp", None, None, None),
            P("section", "dp", None, None, None),
            P("section", "dp", None, None, None),
            P("section", "dp", None, None, None),
        ),
        check_vma=False,
    )
```

```python
import functools

import jax
import jax.numpy as jnp
from jax import lax
from jax.experimental import pallas as pl
from jax.experimental.pallas import tpu as pltpu
from jax.sharding import PartitionSpec as P

MESH = pl.DeviceIdType.MESH
GROUPS = 4

ACROSS = {0: {1: 2, 2: 2}, 1: {1: 0, 2: 4}, 2: {1: 4, 2: 0}, 3: {1: 4, 2: 4}}
ACROSS_QUARTER = {0: {1: 1, 2: 0}, 1: {1: 0, 2: 1}, 2: {1: 1, 2: 0}, 3: {1: 1, 2: 1}}
QUARTERS = 4


def held_at(place):
    return 8 if place == 0 else 4


def base_of(place):
    return 0 if place == 0 else 8 + 4 * (place - 1)


def arrange_kernel(
    owner_ref,
    lengths_ref,
    fa_ref,
    fg_ref,
    la_ref,
    lg_ref,
    first_ref,
    last_ref,
    meta_ref,
    weight,
    held,
    read_sem,
    write_sem,
    place_of,
    count,
):
    docs = lengths_ref.shape[0]
    blocks, _, rows, width = held.shape

    def read(b, n):
        ref = (fa_ref, fg_ref, la_ref, lg_ref)[n]
        span = pl.ds(pl.multiple_of(b * width, width), width)
        return pltpu.make_async_copy(ref.at[0, :, span], held.at[b, n], read_sem.at[b, n])

    def write(b, n):
        ref = (first_ref, first_ref, last_ref, last_ref)[n]
        return pltpu.make_async_copy(held.at[b, n], ref.at[n % 2, place_of[b]], write_sem.at[b, n])

    @pl.loop(0, blocks)
    def _(b):
        for n in range(4):
            read(b, n).start()

    row = lax.broadcasted_iota(jnp.int32, (rows, 128), 0)
    length = jnp.ones((rows, 128), jnp.int32)
    start = jnp.int32(0)
    for d in range(docs):
        size = lengths_ref[d]
        length = jnp.where((row >= start) & (row < start + size), size, length)
        start = start + size
    weight[...] = jnp.sqrt((1.0 / length.astype(jnp.float32)) / jnp.float32(docs * GROUPS))
    for g in range(GROUPS):
        count[g] = 0
    for b in range(blocks):
        owner = owner_ref[b]
        place_of[b] = count[owner]
        count[owner] = count[owner] + 1
    most = jnp.int32(0)
    for g in range(1, GROUPS):
        most = jnp.where(count[g] == 8, jnp.int32(g), most)
    for b in range(blocks):
        place = owner_ref[b] ^ most
        place_of[b] = place_of[b] + jnp.where(place == 0, 0, 4 + 4 * place)
    me = lax.axis_index("dp")
    place = me ^ most
    meta_ref[0] = jnp.where(place == 0, 0, 4 + 4 * place)
    meta_ref[1] = count[me]
    meta_ref[2] = lax.axis_index("section")
    meta_ref[3] = most

    @pl.loop(0, blocks)
    def _(b):
        row_weight = jnp.concatenate([weight[...]] * (width // 128), axis=1)
        for n in range(4):
            read(b, n).wait()
            held[b, n] = (held[b, n].astype(jnp.float32) * row_weight).astype(jnp.bfloat16)
            write(b, n).start()

    @pl.loop(0, blocks)
    def _(b):
        for n in range(4):
            write(b, n).wait()


def arrange(owner, lengths, arrays):
    rows = arrays[0].shape[1]
    blocks = owner.shape[0]
    width = arrays[0].shape[2] // blocks
    hbm = pl.BlockSpec(memory_space=pl.ANY)
    smem = pl.BlockSpec(memory_space=pltpu.SMEM)
    shape = jax.ShapeDtypeStruct((2, 8 + 4 * (GROUPS - 1), rows, width), jnp.bfloat16)
    return pl.pallas_call(
        arrange_kernel,
        in_specs=[smem, smem] + [hbm] * 4,
        out_specs=[hbm, hbm, smem],
        scratch_shapes=[
            pltpu.VMEM((rows, 128), jnp.float32),
            pltpu.VMEM((blocks, 4, rows, width), jnp.bfloat16),
            pltpu.SemaphoreType.DMA((blocks, 4)),
            pltpu.SemaphoreType.DMA((blocks, 4)),
            pltpu.SMEM((blocks,), jnp.int32),
            pltpu.SMEM((GROUPS,), jnp.int32),
        ],
        out_shape=(shape, shape, jax.ShapeDtypeStruct((4,), jnp.int32)),
        compiler_params=pltpu.CompilerParams(vmem_limit_bytes=60 * 2**20),
        name="arrange",
    )(owner, lengths, *arrays)


def exchange_kernel(
    most,
    sections,
    first,
    last,
    got,
    moved,
    early,
    relay,
    relay_quarter,
    send_sem,
    recv_sem,
    move_send,
    move_recv,
    on_send,
    on_recv,
):
    me = lax.axis_index("dp")
    section = lax.axis_index("section")
    plane = section // 2
    core = section - 2 * plane
    has_prev = section > 0
    has_next = section < sections - 1
    planes = sections // 2
    leaving = jnp.where(core == 1, planes - 1 - plane, 0)
    entering = jnp.where((core == 0) & has_prev, planes - plane, 0)

    def role(place):
        def peer(link):
            return {"dp": most ^ place ^ link}

        others = [at for at in range(4) if at != place]

        def move(half, at, quarter=None):
            n = held_at(at) if quarter is None else held_at(at) // QUARTERS
            span = pl.ds(base_of(at) + (0 if quarter is None else quarter * n), n)
            index = 0 if quarter is None else quarter
            return pltpu.make_async_remote_copy(
                src_ref=last.at[half, span],
                dst_ref=moved.at[half, span],
                send_sem=move_send.at[half, at, index],
                recv_sem=move_recv.at[half, at, index],
                device_id={"section": section + 1},
                device_id_type=MESH,
            )

        def go_on(half, quarter):
            m = held_at(place) // QUARTERS
            span = pl.ds(quarter * m, m)
            at = half * QUARTERS + quarter
            return pltpu.make_async_remote_copy(
                src_ref=early.at[half, :, span],
                dst_ref=got.at[2 + half, :, span],
                send_sem=on_send.at[at],
                recv_sem=on_recv.at[at],
                device_id={"section": section + 1},
                device_id_type=MESH,
            )

        class Part:
            def __init__(self, source, target, sem, relay_ref, quarter=None):
                self.source, self.target, self.sem, self.relay = source, target, sem, relay_ref
                self.quarter = quarter
                self.across = ACROSS if quarter is None else ACROSS_QUARTER
                self.sends = [link for link in (1, 2) if self.across[place][link]]
                self.relays = [link for link in (1, 2) if self.across[place ^ link][link]]

            def span(self, to, offset, n, base=0):
                if self.quarter is not None:
                    offset = offset + self.quarter * (held_at(to) // QUARTERS)
                return pl.ds(base + offset, n)

            def size(self, to):
                return held_at(to) if self.quarter is None else held_at(to) // QUARTERS

            def part(self, source_place, link):
                return (0 if link == 1 else self.across[source_place][1]), self.across[source_place][link]

            def copy(self, src, dst, sent, received, link):
                return pltpu.make_async_remote_copy(
                    src_ref=src,
                    dst_ref=dst,
                    send_sem=send_sem.at[self.sem, sent],
                    recv_sem=recv_sem.at[self.sem, received],
                    device_id=peer(link),
                    device_id_type=MESH,
                )

            def direct(self, link):
                to = place ^ link
                n = self.size(to)
                src = self.source.at[self.span(to, 0, n, base_of(to))]
                return self.copy(src, self.target.at[link - 1, self.span(to, 0, n)], link - 1, link - 1, link)

            def hop(self, link):
                offset, n = self.part(place, link)
                to = place ^ 3
                src = self.source.at[self.span(to, offset, n, base_of(to))]
                return self.copy(src, self.relay.at[link - 1, pl.ds(0, n)], 1 + link, 1 + link, link)

            def forward(self, link):
                offset, n = self.part(place ^ link, link)
                out = 3 - link
                to = place ^ out
                dst = self.target.at[2, self.span(to, offset, n)]
                return self.copy(self.relay.at[link - 1, pl.ds(0, n)], dst, 3 + link, 3 + out, out)

            def arrival(self, dst, received):
                return self.copy(dst, dst, received, received, 1)

            def start_hops(self):
                for link in self.sends:
                    self.hop(link).start()

            def start_direct(self):
                for link in (1, 2):
                    self.direct(link).start()

            def pass_on(self):
                for link in self.relays:
                    n = self.part(place ^ link, link)[1]
                    self.arrival(self.relay.at[link - 1, pl.ds(0, n)], 1 + link).wait_recv()
                    self.forward(link).start()

            def wait_arrivals(self):
                n = self.size(place)
                for link in (1, 2):
                    self.arrival(self.target.at[link - 1, self.span(place, 0, n)], link - 1).wait_recv()
                for out in (1, 2):
                    offset, n = self.part(place ^ 3, 3 - out)
                    if n:
                        self.arrival(self.target.at[2, self.span(place, offset, n)], 3 + out).wait_recv()

            def wait_sent(self):
                for link in (1, 2):
                    self.direct(link).wait_send()
                for link in self.sends:
                    self.hop(link).wait_send()
                for link in self.relays:
                    self.forward(link).wait_send()

        def whole(half):
            return Part(first.at[half], got.at[half], half, relay.at[half])

        def late(half, quarter):
            at = half * QUARTERS + quarter
            return Part(moved.at[half], got.at[2 + half], 2 + at, relay_quarter.at[at], quarter)

        def ahead(half, quarter):
            at = (2 + half) * QUARTERS + quarter
            return Part(last.at[half], early.at[half], 2 + at, relay_quarter.at[at], quarter)

        def each(low, high, act):
            for half in range(2):

                @pl.loop(low, high)
                def _(quarter):
                    act(half, quarter)

        barrier = pltpu.get_barrier_semaphore()
        for link in (1, 2):
            pl.semaphore_signal(barrier, inc=1, device_id=peer(link), device_id_type=MESH)

        @pl.when(has_next)
        def _():
            pl.semaphore_signal(barrier, inc=1, device_id={"section": section + 1}, device_id_type=MESH)

        @pl.when(has_prev)
        def _():
            pl.semaphore_signal(barrier, inc=1, device_id={"section": section - 1}, device_id_type=MESH)

        pl.semaphore_wait(barrier, 2 + has_prev.astype(jnp.int32) + has_next.astype(jnp.int32))

        late_from = jnp.where(has_prev, entering, QUARTERS)
        moving_from = jnp.where(has_next, leaving, QUARTERS)

        def start_moves(half, quarter):
            for at in others:
                move(half, at, quarter).start()

        def start_late(half, quarter):
            for at in others:
                move(half, at, quarter).wait_recv()
            late(half, quarter).start_hops()

        def send_on(half, quarter):
            ahead(half, quarter).wait_arrivals()
            go_on(half, quarter).start()

        def wait_moves(half, quarter):
            for at in others:
                move(half, at, quarter).wait_send()

        each(moving_from, QUARTERS, start_moves)
        each(0, leaving, lambda half, quarter: ahead(half, quarter).start_hops())
        for half in range(2):
            whole(half).start_hops()
        each(0, leaving, lambda half, quarter: ahead(half, quarter).start_direct())
        for half in range(2):
            whole(half).start_direct()

        @pl.when(has_next)
        def _():
            for half in range(2):
                move(half, place).start()

        each(0, leaving, lambda half, quarter: ahead(half, quarter).pass_on())
        for half in range(2):
            whole(half).pass_on()
        each(late_from, QUARTERS, start_late)
        each(late_from, QUARTERS, lambda half, quarter: late(half, quarter).start_direct())
        each(0, leaving, send_on)
        each(late_from, QUARTERS, lambda half, quarter: late(half, quarter).pass_on())

        for half in range(2):
            whole(half).wait_arrivals()
        each(late_from, QUARTERS, lambda half, quarter: late(half, quarter).wait_arrivals())
        each(0, entering, lambda half, quarter: go_on(half, quarter).wait_recv())

        @pl.when(has_prev)
        def _():
            for half in range(2):
                move(half, place).wait_recv()

        for half in range(2):
            whole(half).wait_sent()
        each(0, leaving, lambda half, quarter: ahead(half, quarter).wait_sent())
        each(0, leaving, lambda half, quarter: go_on(half, quarter).wait_send())
        each(late_from, QUARTERS, lambda half, quarter: late(half, quarter).wait_sent())
        each(moving_from, QUARTERS, wait_moves)

        @pl.when(has_next)
        def _():
            for half in range(2):
                move(half, place).wait_send()

    for place in range(4):
        pl.when(me == most ^ place)(functools.partial(role, place))


def exchange(most, sections, first, last):
    halves, count, rows, width = first.shape

    def buffer(*lead):
        return jax.ShapeDtypeStruct((*lead, rows, width), jnp.bfloat16)

    hbm = pl.BlockSpec(memory_space=pl.ANY)
    return pl.pallas_call(
        functools.partial(exchange_kernel, most, sections),
        in_specs=[hbm] * 2,
        out_specs=[hbm] * 5,
        out_shape=(
            buffer(4, 3, 8),
            buffer(2, count),
            buffer(2, 3, 8),
            buffer(2, 2, 4),
            buffer(4 * QUARTERS, 2, 1),
        ),
        scratch_shapes=[
            pltpu.SemaphoreType.DMA((2 + 4 * QUARTERS, 6)),
            pltpu.SemaphoreType.DMA((2 + 4 * QUARTERS, 6)),
            pltpu.SemaphoreType.DMA((2, 4, QUARTERS)),
            pltpu.SemaphoreType.DMA((2, 4, QUARTERS)),
            pltpu.SemaphoreType.DMA((2 * QUARTERS,)),
            pltpu.SemaphoreType.DMA((2 * QUARTERS,)),
        ],
        compiler_params=pltpu.CompilerParams(
            collective_id=most, has_side_effects=True, vmem_limit_bytes=60 * 2**20
        ),
        name=f"exchange_{most}",
    )(first, last)


def gram_kernel(meta_ref, own_ref, own_last_ref, got_ref, fa_ref, fg_ref, ca_ref, cg_ref):
    filled = pl.program_id(0) < meta_ref[1]
    has_prev = meta_ref[2] > 0
    contract = (((0,), (0,)), ((), ()))

    def joined(own, half, a):
        return jnp.concatenate([own[half, 0], got_ref[a, 0, 0], got_ref[a, 1, 0], got_ref[a, 2, 0]], axis=0)

    for half, factor_ref, cross_ref in ((0, fa_ref, ca_ref), (1, fg_ref, cg_ref)):

        @pl.when(filled & jnp.logical_not(has_prev))
        def _():
            latter = joined(own_ref, half, half)
            factor_ref[0, 0, 0] = lax.dot_general(latter, latter, contract, preferred_element_type=jnp.float32)

        @pl.when(filled & has_prev)
        def _():
            latter = joined(own_ref, half, half)
            both = jnp.concatenate([latter, joined(own_last_ref, half, 2 + half)], axis=1)
            products = lax.dot_general(both, latter, contract, preferred_element_type=jnp.float32)
            factor_ref[0, 0, 0] = products[: latter.shape[1]]
            cross_ref[0, 0, 0] = products[latter.shape[1] :]

        @pl.when(jnp.logical_not(filled))
        def _():
            factor_ref[...] = jnp.zeros_like(factor_ref)

        @pl.when(jnp.logical_not(filled & has_prev))
        def _():
            cross_ref[...] = jnp.zeros_like(cross_ref)


def grams(meta, first, moved, got):
    slots = got.shape[2]
    rows, width = first.shape[2:]

    def slot_of(i, meta):
        return jnp.minimum(i, jnp.maximum(meta[1] - 1, 0))

    own = pl.BlockSpec((2, 1, rows, width), lambda i, meta: (0, meta[0] + slot_of(i, meta), 0, 0))
    arrived = pl.BlockSpec((4, 3, 1, rows, width), lambda i, meta: (0, 0, slot_of(i, meta), 0, 0))
    out = pl.BlockSpec((1, 1, 1, width, width), lambda i, meta: (0, 0, i, 0, 0))
    shape = jax.ShapeDtypeStruct((1, 1, slots, width, width), jnp.float32)
    return pl.pallas_call(
        gram_kernel,
        grid_spec=pltpu.PrefetchScalarGridSpec(
            num_scalar_prefetch=1, grid=(slots,), in_specs=[own, own, arrived], out_specs=[out] * 4
        ),
        out_shape=(shape,) * 4,
        compiler_params=pltpu.CompilerParams(vmem_limit_bytes=60 * 2**20),
        name="grams",
    )(meta, first, moved, got)


def on_square(first_acts, first_grads, last_acts, last_grads, doc_lengths, block_owner):
    sections = lax.axis_size("section")
    arrays = (first_acts, first_grads, last_acts, last_grads)
    first, last, meta = arrange(block_owner, doc_lengths[0], arrays)

    def branch(which):
        def run(meta, first, last):
            got, moved, *_ = exchange(which, sections, first, last)
            return grams(meta, first, moved, got)

        return run

    return lax.switch(meta[3], [branch(which) for which in range(GROUPS)], meta, first, last)


def shifted(block, axis, distance):
    devices = range(lax.axis_size(axis))
    route = [(i - distance, i) for i in devices if i - distance in devices]
    return lax.ppermute(block, axis, route)


def row_scale(doc_lengths, row_count, docs_all):
    doc_sizes = doc_lengths.astype(jnp.float32)
    doc_end = jnp.cumsum(doc_lengths)
    starts = doc_end - doc_lengths
    places = jnp.arange(row_count, dtype=jnp.int32)
    inside = (places[:, None] >= starts[None, :]) & (places[:, None] < doc_end[None, :])
    inverse = jnp.sum(jnp.where(inside, 1.0 / doc_sizes[None, :], jnp.float32(0.0)), axis=1)
    return jnp.sqrt(inverse / docs_all)


def slot_table(block_owner, groups, slot_count):
    blocks = block_owner.shape[0]
    position = jnp.arange(blocks, dtype=jnp.int32)
    same_owner = block_owner[:, None] == block_owner[None, :]
    earlier = position[None, :] < position[:, None]
    slot_index = jnp.sum(jnp.where(same_owner & earlier, 1, 0), axis=1).astype(jnp.int32)
    target = block_owner * slot_count + slot_index
    wanted = jnp.arange(groups * slot_count, dtype=jnp.int32)
    return jnp.where(wanted[:, None] == target[None, :], 1.0, 0.0).astype(jnp.bfloat16)


def into_slots(matrix, selector, groups, slot_count):
    row_count, widths = matrix.shape
    blocks = selector.shape[1]
    block_width = widths // blocks
    blocked = matrix.reshape(row_count, blocks, block_width)
    placed = jnp.einsum("cb,rbf->crf", selector, blocked, preferred_element_type=jnp.float32)
    return placed.astype(jnp.bfloat16).reshape(groups, slot_count, row_count, block_width)


def owner_gram(former, latter):
    return jnp.einsum("gkrf,gkrh->kfh", former, latter, preferred_element_type=jnp.float32)


def on_device(first_acts, first_grads, last_acts, last_grads, doc_lengths, block_owner):
    row_count = first_acts.shape[1]
    groups = lax.axis_size("dp")
    blocks = block_owner.shape[0]
    slot_count = 2 * blocks // groups
    row_weight = row_scale(doc_lengths[0], row_count, doc_lengths.shape[1] * groups)[:, None]

    def weighted(matrix):
        return (matrix[0].astype(jnp.float32) * row_weight).astype(jnp.bfloat16)

    own_acts = weighted(first_acts)
    own_grads = weighted(first_grads)
    tail_acts = weighted(last_acts)
    tail_grads = weighted(last_grads)
    selector = slot_table(block_owner, groups, slot_count)
    acts_in = lax.all_to_all(
        into_slots(own_acts, selector, groups, slot_count),
        "dp",
        split_axis=0,
        concat_axis=0,
        tiled=True,
    )
    grads_in = lax.all_to_all(
        into_slots(own_grads, selector, groups, slot_count),
        "dp",
        split_axis=0,
        concat_axis=0,
        tiled=True,
    )
    tail_in = lax.all_to_all(
        into_slots(tail_acts, selector, groups, slot_count),
        "dp",
        split_axis=0,
        concat_axis=0,
        tiled=True,
    )
    tail_grad_in = lax.all_to_all(
        into_slots(tail_grads, selector, groups, slot_count),
        "dp",
        split_axis=0,
        concat_axis=0,
        tiled=True,
    )
    prev_in, prev_grad_in = shifted((tail_in, tail_grad_in), "section", 1)
    first = owner_gram(acts_in, acts_in)
    second = owner_gram(grads_in, grads_in)
    third = owner_gram(prev_in, acts_in)
    fourth = owner_gram(prev_grad_in, grads_in)
    results = (first[None, None], second[None, None], third[None, None], fourth[None, None])
    return results


def solution(mesh):
    placed = (
        P("section", "dp", None),
        P("section", "dp", None),
        P("section", "dp", None),
        P("section", "dp", None),
        P("dp", None),
        P(),
    )
    return jax.shard_map(
        on_square if mesh.shape["dp"] == GROUPS else on_device,
        mesh=mesh,
        in_specs=placed,
        out_specs=(
            P("section", "dp", None, None, None),
            P("section", "dp", None, None, None),
            P("section", "dp", None, None, None),
            P("section", "dp", None, None, None),
        ),
        check_vma=False,
    )
```
